32 devices in a mesh: case: 2 (over x), span: 16 (over z, y, core).
Axes of the slice: x: 2, y: 2, z: 4, core: 2. Of those that a mesh axis runs over, the one named last changes fastest.
Arguments:
- adjoint_in: float32 [38, 16, 128, 128], P('case', 'span'), parts along dimension 0, may hold values from -6 to 6
- density: float32 [4, 16, 128, 128], P('case', 'span'), parts along dimension 0, may hold values from 0.8 to 1.2
- velocity: float32 [4, 3, 16, 128, 128], P('case', None, 'span'), parts along dimension 0, may hold values from -0.25 to 0.25
- links: int32 [2, 32, 128, 128], P(None, ('case', 'span')), parts along dimension 1, may hold values from 0 to 1023, as said below
- patch_map: int32 [32, 128, 128], P(('case', 'span')), parts along dimension 0, may hold values from 0 to 4095
- owner: int32 [4096], replicated, may hold values from 0 to 4095, each once
- relax: float32 [38], P('case'), parts along dimension 0, may hold values from 0.5 to 1.9
Outputs:
- adjoint_out: float32 [38, 16, 128, 128], P('case', 'span'), parts along dimension 0
- patch_gradient: float32 [8192], P(('case', 'span')), parts along dimension 0
The draws below stay inside these ranges and needn't reach their ends.
There are 2 independent parts, one for each index of `case`. The reference program is written for one: setup_inputs(seed, part) draws one part's arguments, and reference() takes and returns one part's arrays. A program takes and returns all parts, laid end to end along the dimension named above; an argument that names none is the same for every part. Nothing has to cross between parts.
Inputs may be any that keep to these rules, and one draw needn't show every extreme that they name: `links`: bit j of a cell (held in plane j // 10 at position j mod 10) is set exactly when the cell at x + c_j is solid (bit 0: the cell itself); cells beyond the cross-section count as solid, the span is periodic. The solid body is a cylinder with a helical fillet. `patch_map`: patch of every cell; only cells with some link bit set contribute.
All inputs are finite; a program needn't handle non-finite values.
Results may differ from the reference program's by a relative error of at most 0.00013.
Values sent between devices are 32-bit elements; how exact they have to be, the bound alone decides.
A program may use at most 64 MiB of HBM per device.

```python
import math
import jax
import jax.numpy as jnp
from jax import lax

Q = 19
LEVELS = 2
NY = 128
NZ = 128
PATCHES = 4096
NX = 16


def draw_links(key, part):
    local_key = jax.random.fold_in(key, 11)
    first_key, second_key = jax.random.split(local_key)
    pitch_cells = jax.random.randint(first_key, (), 2, 7)
    phase_index = jax.random.randint(second_key, (), 0, 8)
    radius = min(NY, NZ) // 5
    planes = jnp.arange(NX, dtype=jnp.int32)[:, None, None]
    across_y = jnp.arange(NY, dtype=jnp.int32)[None, :, None] - NY // 2
    across_z = jnp.arange(NZ, dtype=jnp.int32)[None, None, :] - NZ // 2
    core = across_y * across_y + across_z * across_z < radius * radius
    offset_y = jnp.array([10, 7, 0, -7, -10, -7, 0, 7], dtype=jnp.int32)
    offset_z = jnp.array([0, 7, 10, 7, 0, -7, -10, -7], dtype=jnp.int32)
    sector = (planes // pitch_cells + phase_index) % 8
    fillet_y = jnp.take(offset_y, sector) * radius // 10
    fillet_z = jnp.take(offset_z, sector) * radius // 10
    delta_y = across_y - fillet_y
    delta_z = across_z - fillet_z
    fillet = delta_y * delta_y + delta_z * delta_z < max(radius * radius // 9, 2)
    solid = jnp.logical_or(core, fillet).astype(jnp.int32)
    padded = jnp.pad(solid, ((0, 0), (1, 1), (1, 1)), constant_values=1)
    velocity_list = [[0, 0, 0], [1, 0, 0], [-1, 0, 0], [0, 1, 0], [0, -1, 0], [0, 0, 1], [0, 0, -1], [1, 1, 0], [-1, -1, 0], [1, -1, 0], [-1, 1, 0], [1, 0, 1], [-1, 0, -1], [1, 0, -1], [-1, 0, 1], [0, 1, 1], [0, -1, -1], [0, 1, -1], [0, -1, 1]]
    low_bits = jnp.zeros((NX, NY, NZ), jnp.int32)
    high_bits = jnp.zeros((NX, NY, NZ), jnp.int32)
    for direction in range(19):
        step_x, step_y, step_z = velocity_list[direction]
        rolled = jnp.roll(padded, -step_x, axis=0)
        neighbour = rolled[:, 1 + step_y:1 + step_y + NY, 1 + step_z:1 + step_z + NZ]
        if direction < 10:
            low_bits = low_bits + neighbour * 2 ** direction
        else:
            high_bits = high_bits + neighbour * 2 ** (direction - 10)
    return jnp.stack([low_bits, high_bits]).astype(jnp.int32)


def touch_ends(values, stream_key, smallest, top_value):
    longest = values.shape.index(max(values.shape))
    spots = []
    for shift in (0, 1):
        where = [jax.random.randint(jax.random.fold_in(stream_key, axis), (), 0, length) for axis, length in enumerate(values.shape)]
        where[longest] = (where[longest] + shift) % values.shape[longest]
        spots.append(tuple(where))
    return values.at[spots[0]].set(smallest).at[spots[1]].set(top_value)


def block_scale(stream_key, shape, cuts, low, top_value):
    gain, own = 1.0, jax.random.fold_in(stream_key, 6)
    for position, parts in cuts:
        steps = jnp.exp(jax.random.uniform(jax.random.fold_in(own, position), (parts,), jnp.float32, low / len(cuts), top_value / len(cuts)))
        gain = gain * jnp.repeat(steps, shape[position] // parts).reshape([-1 if axis == position else 1 for axis in range(len(shape))])
    return gain


def normal_values(own_key, extent, scale, reach, cuts=(), kind=jnp.bfloat16):
    values = jax.random.normal(own_key, extent, jnp.float32) * scale
    if len(cuts) > 0:
        values = block_scale(own_key, extent, cuts, -0.22, 0.18) * values
    return jnp.clip(values, min=-reach, max=reach).astype(kind)


def setup_inputs(seed: int = 0, part: int = 0) -> dict:
    streams_of = jax.random.split(jax.random.key(seed), 8)
    part_keys = jax.random.split(jax.random.fold_in(streams_of[7], part), 8)
    adjoint_in = normal_values(part_keys[0], (Q, NX, NY, NZ), 1.0, 6.0, ((1, 16),), jnp.float32)
    density = jnp.clip(0.8 + 0.40000004 * jax.random.uniform(part_keys[1], (LEVELS, NX, NY, NZ), jnp.float32) ** block_scale(part_keys[1], (LEVELS, NX, NY, NZ), ((1, 16),), -0.2, 0.2), 0.8, 1.2)
    velocity = normal_values(part_keys[2], (LEVELS, 3, NX, NY, NZ), 0.05, 0.25, ((2, 16),), jnp.float32)
    links = draw_links(jax.random.fold_in(jax.random.fold_in(streams_of[7], part), 71), part)
    patch_map = touch_ends(jax.random.randint(part_keys[4], (NX, NY, NZ), 0, PATCHES), jax.random.fold_in(part_keys[4], 1), 0, PATCHES - 1).astype(jnp.int32)
    owner = jax.random.permutation(streams_of[5], PATCHES).astype(jnp.int32)
    relax = jnp.clip(jnp.exp(jax.random.uniform(part_keys[6], (Q,), jnp.float32, math.log(0.5), math.log(1.9))), 0.5, 1.9)
    return {"adjoint_in": adjoint_in, "density": density, "velocity": velocity, "links": links, "patch_map": patch_map, "owner": owner, "relax": relax}


def lattice_tables():
    velocities = [[0, 0, 0], [1, 0, 0], [-1, 0, 0], [0, 1, 0], [0, -1, 0], [0, 0, 1], [0, 0, -1], [1, 1, 0], [-1, -1, 0], [1, -1, 0], [-1, 1, 0], [1, 0, 1], [-1, 0, -1], [1, 0, -1], [-1, 0, 1], [0, 1, 1], [0, -1, -1], [0, 1, -1], [0, -1, 1]]
    weights = [1.0 / 3.0] + [1.0 / 18.0] * 6 + [1.0 / 36.0] * 12
    opposite = [0, 2, 1, 4, 3, 6, 5, 8, 7, 10, 9, 12, 11, 14, 13, 16, 15, 18, 17]
    lattice = jnp.asarray(velocities, jnp.float32)
    along_x = lattice[:, 0]
    along_y = lattice[:, 1]
    along_z = lattice[:, 2]
    monomials = [jnp.ones((19,), jnp.float32), along_x, along_y, along_z, along_x * along_y, along_x * along_z, along_y * along_z, along_x * along_x, along_y * along_y, along_z * along_z, along_x * along_y * along_y, along_x * along_z * along_z, along_y * along_x * along_x, along_z * along_x * along_x, along_y * along_z * along_z, along_z * along_y * along_y, along_x * along_x * along_y * along_y, along_x * along_x * along_z * along_z, along_y * along_y * along_z * along_z]
    basis = []
    for column in monomials:
        vector = column
        for sweep in range(2):
            for earlier in basis:
                vector = vector - jnp.sum(vector * earlier) * earlier
        vector = vector / jnp.sqrt(jnp.sum(vector * vector))
        basis.append(vector)
    return (velocities, weights, opposite, jnp.stack(basis))

def link_bit(links, direction):
    return jnp.bitwise_and(jnp.right_shift(links[direction // 10], direction % 10), 1)

def shift_cross(plane, step_y, step_z):
    padded = jnp.pad(plane, ((0, 0), (1, 1), (1, 1)))
    return padded[:, 1 + step_y:1 + step_y + plane.shape[1], 1 + step_z:1 + step_z + plane.shape[2]]

def collide_adjoint(propagated, density, velocity, fluid_mask, relax_rates):
    velocities, weights, opposite, moment_table = lattice_tables()
    highest = lax.Precision.HIGHEST
    full_shape = propagated.shape
    flattened = propagated.reshape(19, -1)
    flow_flat = velocity.reshape(3, -1)
    moment_matrix = moment_table
    lattice = jnp.asarray(velocities, jnp.float32)
    moments = jnp.dot(moment_matrix, flattened, precision=highest)
    relaxed = jnp.dot(moment_matrix.T, relax_rates[:, None] * moments, precision=highest)
    projected = jnp.dot(lattice, flow_flat, precision=highest)
    speed_sq = lax.optimization_barrier(jnp.sum(flow_flat * flow_flat, axis=0))
    weighted = jnp.asarray(weights, jnp.float32)[:, None] * relaxed
    scalar_part = lax.optimization_barrier(jnp.sum(weighted * (1.0 - 4.5 * projected * projected + 1.5 * speed_sq[None, :]), axis=0))
    vector_part = 3.0 * jnp.dot(lattice.T, weighted * (1.0 + 3.0 * projected), precision=highest) - 3.0 * flow_flat * lax.optimization_barrier(jnp.sum(weighted, axis=0))[None, :]
    result = flattened - relaxed + scalar_part[None, :] + jnp.dot(lattice, vector_part, precision=highest)
    return (fluid_mask.reshape(1, -1) * result).reshape(full_shape)

def reverse_step(adjoint, links, density, velocity, relax_rates):
    velocities, weights, opposite, moment_table = lattice_tables()
    fluid_mask = (1 - link_bit(links, 0)).astype(jnp.float32)
    speed_sq = lax.optimization_barrier(jnp.sum(velocity * velocity, axis=0))
    propagated = []
    wall_term = jnp.zeros(links.shape[1:], jnp.float32)
    for direction in range(19):
        step_x = velocities[direction][0]
        step_y = velocities[direction][1]
        step_z = velocities[direction][2]
        linked = link_bit(links, direction).astype(jnp.float32)
        upstream = shift_cross(jnp.roll(adjoint[direction], -step_x, axis=0), step_y, step_z)
        reflected = adjoint[opposite[direction]]
        propagated.append(fluid_mask * ((1.0 - linked) * upstream + linked * reflected))
        along = step_x * velocity[0] + step_y * velocity[1] + step_z * velocity[2]
        equilibrium = density * (1.0 + 3.0 * along + 4.5 * along * along - 1.5 * speed_sq)
        wall_term = wall_term + fluid_mask * linked * equilibrium * reflected
    propagated = jnp.stack(propagated)
    planes = propagated.shape[1]
    block_len = planes // 8
    pieces = []
    for block_index in range(8):
        begin = block_index * block_len
        finish = begin + block_len
        pieces.append(collide_adjoint(propagated[:, begin:finish], density[begin:finish], velocity[:, begin:finish], fluid_mask[begin:finish], relax_rates))
    return (jnp.concatenate(pieces, axis=1), wall_term)

def reference(adjoint_in, density, velocity, links, patch_map, owner, relax):
    relax_rates = relax * (jnp.arange(19) >= 4).astype(jnp.float32)
    adjoint = adjoint_in
    wall_total = jnp.zeros(links.shape[1:], jnp.float32)
    for time_level in (1, 0):
        adjoint, wall_term = reverse_step(adjoint, links, density[time_level], velocity[time_level], relax_rates)
        wall_total = wall_total + wall_term
    target_rows = jnp.take(owner, patch_map)
    gradient = jax.ops.segment_sum(wall_total.reshape(-1), target_rows.reshape(-1).astype(jnp.int32), num_segments=owner.shape[0])
    return (adjoint, gradient)
```

```python
import functools

import jax
import jax.numpy as jnp
import numpy as np
from jax import lax
from jax.experimental import pallas as pl
from jax.experimental.pallas import tpu as pltpu
from jax.sharding import PartitionSpec as P

MESH = pl.DeviceIdType.MESH
RISING = (1, 7, 9, 11, 13)
FALLING = (2, 8, 10, 12, 14)
OPPOSITE = (0, 2, 1, 4, 3, 6, 5, 8, 7, 10, 9, 12, 11, 14, 13, 16, 15, 18, 17)
VELOCITIES = (
    (0, 0, 0),
    (1, 0, 0),
    (-1, 0, 0),
    (0, 1, 0),
    (0, -1, 0),
    (0, 0, 1),
    (0, 0, -1),
    (1, 1, 0),
    (-1, -1, 0),
    (1, -1, 0),
    (-1, 1, 0),
    (1, 0, 1),
    (-1, 0, -1),
    (1, 0, -1),
    (-1, 0, 1),
    (0, 1, 1),
    (0, -1, -1),
    (0, 1, -1),
    (0, -1, 1),
)
PAD = 8
ROWS = 8


def moment_table():
    lattice = np.asarray(VELOCITIES, np.float32)
    x, y, z = lattice[:, 0], lattice[:, 1], lattice[:, 2]
    monomials = [np.ones((19,), np.float32), x, y, z, x * y, x * z, y * z, x * x, y * y, z * z]
    monomials += [x * y * y, x * z * z, y * x * x, z * x * x, y * z * z, z * y * y]
    monomials += [x * x * y * y, x * x * z * z, y * y * z * z]
    basis = []
    for vector in monomials:
        for sweep in range(2):
            for earlier in basis:
                vector = vector - np.sum(vector * earlier) * earlier
        basis.append(vector / np.sqrt(np.sum(vector * vector)))
    return np.stack(basis)


TABLE = moment_table()
EVEN_AT = (0, 1, 3, 5, 7, 11, 15)
EVEN_ROWS = (7, 8, 9, 16, 17, 18)
ODD_AT = ((1, 7, 11), (3, 7, 15), (5, 11, 15))
ODD_ROWS = ((10, 11), (12, 14), (13, 15))
MIXED = ((4, 7), (5, 11), (6, 15))


def coefficients(relax_ref):
    def block(at, rows):
        rates = [relax_ref[row] for row in rows]
        out = {}
        for a in range(len(at)):
            for b in range(a, len(at)):
                total = None
                for row, rate in zip(rows, rates):
                    factor = float(TABLE[row, at[a]]) * float(TABLE[row, at[b]])
                    if abs(factor) < 1e-6:
                        continue
                    term = rate * np.float32(factor)
                    total = term if total is None else total + term
                out[a, b] = out[b, a] = total
        return out

    even = block(EVEN_AT, EVEN_ROWS)
    odd = [block(at, rows) for at, rows in zip(ODD_AT, ODD_ROWS)]
    mixed = [relax_ref[row] * np.float32(float(TABLE[row, at]) ** 2) for row, at in MIXED]
    return even, odd, mixed


def apply(block, values):
    result = []
    for a in range(len(values)):
        total = None
        for b, value in enumerate(values):
            if block[a, b] is None:
                continue
            term = block[a, b] * value
            total = term if total is None else total + term
        result.append(total)
    return result


def classes(p):
    even = [p[0], p[1] + p[2], p[3] + p[4], p[5] + p[6]]
    single = [p[1] - p[2], p[3] - p[4], p[5] - p[6]]
    mixed, firsts, seconds = [], [], []
    for base in (7, 11, 15):
        a, b = p[base] + p[base + 1], p[base + 2] + p[base + 3]
        c, d = p[base] - p[base + 1], p[base + 2] - p[base + 3]
        even.append(a + b)
        mixed.append(a - b)
        firsts.append(c + d)
        seconds.append(c - d)
    odd = [
        [single[0], firsts[0], firsts[1]],
        [single[1], seconds[0], firsts[2]],
        [single[2], seconds[1], seconds[2]],
    ]
    return even, odd, mixed


def quadratic(diagonal, mixed, u):
    xx, yy, zz = diagonal
    xy, xz, yz = mixed
    return (
        u[0] * xx + u[1] * xy + u[2] * xz,
        u[0] * xy + u[1] * yy + u[2] * yz,
        u[0] * xz + u[1] * yz + u[2] * zz,
    )


def collide(p, u, fluid, coefs):
    even_block, odd_block, mixed_block = coefs
    even, odd, mixed = classes(p)
    ge = apply(even_block, even)
    go = [apply(block, values) for block, values in zip(odd_block, odd)]
    gm = [scale * value for scale, value in zip(mixed_block, mixed)]
    w0, w1, w2 = np.float32(1 / 3), np.float32(2 / 18), np.float32(4 / 36)
    axes = [w1 * value for value in ge[1:4]]
    planes = [w2 * value for value in ge[4:7]]
    diagonal = (
        axes[0] + (planes[0] + planes[1]),
        axes[1] + (planes[0] + planes[2]),
        axes[2] + (planes[1] + planes[2]),
    )
    total = w0 * ge[0] + (axes[0] + axes[1] + axes[2]) + (planes[0] + planes[1] + planes[2])
    first = [w1 * value[0] + w2 * (value[1] + value[2]) for value in go]
    cross = [w2 * value for value in gm]
    bent = quadratic(diagonal, cross, u)
    speed_sq = u[0] * u[0] + u[1] * u[1] + u[2] * u[2]
    s0 = total * (1.0 + 1.5 * speed_sq) - 4.5 * (u[0] * bent[0] + u[1] * bent[1] + u[2] * bent[2])
    s = [3.0 * (first[i] + 3.0 * bent[i] - u[i] * total) for i in range(3)]
    he = [s0 - value for value in ge]
    ho = [[s[i] - value for value in go[i]] for i in range(3)]
    out = [None] * 19
    out[0] = p[0] + he[0]
    for i in range(3):
        out[1 + 2 * i] = p[1 + 2 * i] + (he[1 + i] + ho[i][0])
        out[2 + 2 * i] = p[2 + 2 * i] + (he[1 + i] - ho[i][0])
    pairs = ((ho[0][1], ho[1][1]), (ho[0][2], ho[2][1]), (ho[1][2], ho[2][2]))
    for i, (left, right) in enumerate(pairs):
        base = 7 + 4 * i
        e, f = he[4 + i] - gm[i], he[4 + i] + gm[i]
        x, y = left + right, left - right
        out[base] = p[base] + (e + x)
        out[base + 1] = p[base + 1] + (e - x)
        out[base + 2] = p[base + 2] + (f + y)
        out[base + 3] = p[base + 3] + (f - y)
    return [jnp.where(fluid, value, 0.0) for value in out]


def wall_value(x, rho, u, fluid):
    even, odd, mixed = classes(x)
    total = sum(even[1:], even[0])
    diagonal = (
        even[1] + (even[4] + even[5]),
        even[2] + (even[4] + even[6]),
        even[3] + (even[5] + even[6]),
    )
    first = [value[0] + (value[1] + value[2]) for value in odd]
    bent = quadratic(diagonal, mixed, u)
    speed_sq = u[0] * u[0] + u[1] * u[1] + u[2] * u[2]
    linear = [3.0 * first[i] + 4.5 * bent[i] for i in range(3)]
    value = total * (1.0 - 1.5 * speed_sq) + (
        u[0] * linear[0] + u[1] * linear[1] + u[2] * linear[2]
    )
    return jnp.where(fluid, rho * value, 0.0)


def split3(value):
    one = value.astype(jnp.bfloat16)
    rest = value - one.astype(jnp.float32)
    two = rest.astype(jnp.bfloat16)
    three = (rest - two.astype(jnp.float32)).astype(jnp.bfloat16)
    return [part.astype(jnp.float32) for part in (one, two, three)]


def one_hot_sums(index, value, low_bits, highs):
    high = lax.shift_right_logical(index, low_bits)
    low = lax.bitwise_and(index, (1 << low_bits) - 1)
    parts = split3(value)
    high_iota = lax.broadcasted_iota(jnp.int32, (highs, 128), 0)
    low_iota = lax.broadcasted_iota(jnp.int32, (128, 128), 0)
    lefts, rights = [], []
    for row in range(ROWS):
        hit = high_iota == high[row : row + 1, :]
        left = [jnp.where(hit, part[row : row + 1, :], 0.0) for part in parts]
        lefts.append(jnp.concatenate(left, axis=0).astype(jnp.bfloat16))
        right = jnp.where(low_iota == low[row : row + 1, :], 1.0, 0.0)
        rights.append(right.astype(jnp.bfloat16))
    return lax.dot_general(
        jnp.concatenate(lefts, axis=1),
        jnp.concatenate(rights, axis=1),
        (((1,), (1,)), ((), ())),
        preferred_element_type=jnp.float32,
    )


def kernel(
    n,
    low_bits,
    relax_ref,
    adjoint_ref,
    density_ref,
    velocity_ref,
    links_ref,
    patch_ref,
    owner_ref,
    out_ref,
    gradient_ref,
    first,
    second,
    rims_one,
    rims_two,
    rho,
    flow,
    bits,
    patch,
    owner,
    wall,
    sums,
    outgoing,
    incoming,
    local_sem,
    send_one,
    recv_one,
    send_two,
    recv_two,
    send_sum,
    recv_sum,
):
    me = lax.axis_index("span")
    above, below = lax.rem(me + 1, n), lax.rem(me + n - 1, n)
    ny = wall.shape[0]
    chunks = ny // ROWS

    def other(d):
        return lax.rem(me + d, n)

    loads = [
        pltpu.make_async_copy(source, target, local_sem.at[i])
        for i, (source, target) in enumerate(
            (
                (adjoint_ref.at[:, 0], first.at[:, pl.ds(PAD, ny), :]),
                (links_ref.at[:, 0], bits),
                (velocity_ref.at[:, :, 0], flow),
                (density_ref.at[:, 0], rho),
                (patch_ref.at[0], patch),
                (owner_ref, owner),
            )
        )
    ]
    for load in loads:
        load.start()

    barrier = pltpu.get_barrier_semaphore()

    def greet(d, carry):
        pl.semaphore_signal(barrier, inc=1, device_id={"span": other(d)}, device_id_type=MESH)
        return carry

    lax.fori_loop(1, n, greet, 0)
    for buffer in (first, second, rims_one, rims_two):
        blank = jnp.zeros((buffer.shape[0], PAD, buffer.shape[2]), jnp.float32)
        buffer[:, 0:PAD, :] = blank
        buffer[:, PAD + ny : PAD + ny + PAD, :] = blank
    pl.semaphore_wait(barrier, n - 1)

    def exchange(plane_of, rims, send_sem, recv_sem):
        copies = []
        for k in range(5):
            for slot, direction, target in ((k, RISING[k], below), (5 + k, FALLING[k], above)):
                copies.append(
                    pltpu.make_async_remote_copy(
                        src_ref=plane_of(direction),
                        dst_ref=rims.at[slot, pl.ds(PAD, ny), :],
                        send_sem=send_sem.at[slot],
                        recv_sem=recv_sem.at[slot],
                        device_id={"span": target},
                        device_id_type=MESH,
                    )
                )
        for copy in copies:
            copy.start()
        return copies

    copies_one = exchange(lambda j: adjoint_ref.at[j, 0], rims_one, send_one, recv_one)
    coefs = coefficients(relax_ref)
    for load in loads:
        load.wait()

    def masks(rows):
        low, high = bits[0, rows, :], bits[1, rows, :]
        return [
            lax.bitwise_and(low if j < 10 else high, 1 << (j % 10)) != 0 for j in range(19)
        ]

    def walls(level, populations, add):
        def step(i, carry):
            start = pl.multiple_of(i * ROWS, ROWS)
            rows = pl.ds(start, ROWS)
            inner = pl.ds(pl.multiple_of(start + PAD, ROWS), ROWS)
            linked = masks(rows)
            u = [flow[level, axis, rows, :] for axis in range(3)]
            x = [
                jnp.where(linked[j], populations[OPPOSITE[j], inner, :], 0.0) for j in range(19)
            ]
            value = wall_value(x, rho[level, rows, :], u, jnp.logical_not(linked[0]))
            wall[rows, :] = wall[rows, :] + value if add else value
            return carry

        lax.fori_loop(0, chunks, step, 0)

    def collisions(level, populations, rims, store):
        def step(i, carry):
            start = pl.multiple_of(i * ROWS, ROWS)
            rows = pl.ds(start, ROWS)
            inner = pl.ds(pl.multiple_of(start + PAD, ROWS), ROWS)
            linked = masks(rows)
            u = [flow[level, axis, rows, :] for axis in range(3)]
            p = []
            for j, (step_x, step_y, step_z) in enumerate(VELOCITIES):
                shifted = inner if step_y == 0 else pl.ds(start + (PAD + step_y), ROWS)
                if step_x == 1:
                    upstream = rims[RISING.index(j), shifted, :]
                elif step_x == -1:
                    upstream = rims[5 + FALLING.index(j), shifted, :]
                else:
                    upstream = populations[j, shifted, :]
                if step_z != 0:
                    upstream = pltpu.roll(upstream, (-step_z) % upstream.shape[1], 1)
                p.append(jnp.where(linked[j], populations[OPPOSITE[j], inner, :], upstream))
            for j, value in enumerate(collide(p, u, jnp.logical_not(linked[0]), coefs)):
                store(j, rows, inner, value)
            return carry

        lax.fori_loop(0, chunks, step, 0)

    walls(1, first, False)
    for copy in copies_one:
        copy.wait_recv()

    def store_second(j, rows, inner, value):
        second[j, inner, :] = value

    collisions(1, first, rims_one, store_second)
    copies_two = exchange(lambda j: second.at[j, pl.ds(PAD, ny), :], rims_two, send_two, recv_two)

    walls(0, second, True)

    def by_patch(i, total):
        rows = pl.ds(pl.multiple_of(i * ROWS, ROWS), ROWS)
        return total + one_hot_sums(patch[rows, :], wall[rows, :], 7, owner.shape[0])

    highs = owner.shape[0]
    total = lax.fori_loop(0, chunks, by_patch, jnp.zeros((3 * highs, 128), jnp.float32))
    sums[...] = total[:highs] + (total[highs : 2 * highs] + total[2 * highs :])

    targets = outgoing.shape[0] * outgoing.shape[1]

    def by_owner(i, total):
        rows = pl.ds(pl.multiple_of(i * ROWS, ROWS), ROWS)
        return total + one_hot_sums(owner[rows, :], sums[rows, :], low_bits, targets)

    total = lax.fori_loop(
        0, highs // ROWS, by_owner, jnp.zeros((3 * targets, 128), jnp.float32)
    )
    placed = total[:targets] + (total[targets : 2 * targets] + total[2 * targets :])
    per = outgoing.shape[1]
    for i in range(n):
        outgoing[i] = placed[i * per : (i + 1) * per]

    def sum_copy(d, source):
        return pltpu.make_async_remote_copy(
            src_ref=outgoing.at[other(d)],
            dst_ref=incoming.at[source],
            send_sem=send_sum.at[d],
            recv_sem=recv_sum.at[source],
            device_id={"span": other(d)},
            device_id_type=MESH,
        )

    def send(d, carry):
        sum_copy(d, me).start()
        return carry

    lax.fori_loop(1, n, send, 0)

    for copy in copies_two:
        copy.wait_recv()

    def store_out(j, rows, inner, value):
        out_ref[j, 0, rows, :] = value

    collisions(0, second, rims_two, store_out)

    def collect(d, total):
        source = other(n - d)
        sum_copy(d, source).wait_recv()
        return total + incoming[source]

    gradient_ref[...] = lax.fori_loop(1, n, collect, outgoing[me])

    def sent(d, carry):
        sum_copy(d, me).wait_send()
        return carry

    lax.fori_loop(1, n, sent, 0)
    for copy in copies_one + copies_two:
        copy.wait_send()


def body(n, adjoint_in, density, velocity, links, patch_map, owner, relax):
    _, planes, ny, nz = adjoint_in.shape
    assert planes == 1 and nz == 128 and ny % ROWS == 0
    rows = owner.shape[0] // n
    low = min(128, rows)
    per = rows // low
    highs = owner.shape[0] // 128
    padded = ny + 2 * PAD
    hbm = pl.BlockSpec(memory_space=pl.ANY)
    vmem = pl.BlockSpec(memory_space=pltpu.VMEM)
    levels = density.shape[0]
    adjoint, gradient = pl.pallas_call(
        functools.partial(kernel, n, low.bit_length() - 1),
        out_shape=(
            jax.ShapeDtypeStruct(adjoint_in.shape, jnp.float32),
            jax.ShapeDtypeStruct((per, 128), jnp.float32),
        ),
        in_specs=[pl.BlockSpec(memory_space=pltpu.SMEM)] + [hbm] * 6,
        out_specs=(vmem, vmem),
        scratch_shapes=[
            pltpu.VMEM((19, padded, nz), jnp.float32),
            pltpu.VMEM((19, padded, nz), jnp.float32),
            pltpu.VMEM((10, padded, nz), jnp.float32),
            pltpu.VMEM((10, padded, nz), jnp.float32),
            pltpu.VMEM((levels, ny, nz), jnp.float32),
            pltpu.VMEM((levels, 3, ny, nz), jnp.float32),
            pltpu.VMEM((2, ny, nz), jnp.int32),
            pltpu.VMEM((ny, nz), jnp.int32),
            pltpu.VMEM((highs, 128), jnp.int32),
            pltpu.VMEM((ny, nz), jnp.float32),
            pltpu.VMEM((highs, 128), jnp.float32),
            pltpu.VMEM((n, per, 128), jnp.float32),
            pltpu.VMEM((n, per, 128), jnp.float32),
            pltpu.SemaphoreType.DMA((6,)),
            pltpu.SemaphoreType.DMA((10,)),
            pltpu.SemaphoreType.DMA((10,)),
            pltpu.SemaphoreType.DMA((10,)),
            pltpu.SemaphoreType.DMA((10,)),
            pltpu.SemaphoreType.DMA((n,)),
            pltpu.SemaphoreType.DMA((n,)),
        ],
        compiler_params=pltpu.CompilerParams(
            collective_id=0, has_side_effects=True, vmem_limit_bytes=32 * 1024 * 1024
        ),
        cost_estimate=pl.CostEstimate(
            flops=40_000_000, bytes_accessed=4_000_000, transcendentals=0
        ),
    )(relax, adjoint_in, density, velocity, links, patch_map, owner.reshape(highs, 128))
    return adjoint, gradient[:, :low].reshape(rows)


def solution(mesh):
    in_specs = (
        P("case", "span", None, None),
        P("case", "span", None, None),
        P("case", None, "span", None, None),
        P(None, ("case", "span"), None, None),
        P(("case", "span"), None, None),
        P(),
        P("case"),
    )
    out_specs = (P("case", "span", None, None), P(("case", "span")))
    return jax.shard_map(
        functools.partial(body, mesh.shape["span"]),
        mesh=mesh,
        in_specs=in_specs,
        out_specs=out_specs,
        check_vma=False,
    )
```

```python
import functools

import jax
import jax.numpy as jnp
import numpy as np
from jax import lax
from jax.experimental import pallas as pl
from jax.experimental.pallas import tpu as pltpu
from jax.sharding import PartitionSpec as P

MESH = pl.DeviceIdType.MESH
RISING = (1, 7, 9, 11, 13)
FALLING = (2, 8, 10, 12, 14)
OPPOSITE = (0, 2, 1, 4, 3, 6, 5, 8, 7, 10, 9, 12, 11, 14, 13, 16, 15, 18, 17)
VELOCITIES = (
    (0, 0, 0),
    (1, 0, 0),
    (-1, 0, 0),
    (0, 1, 0),
    (0, -1, 0),
    (0, 0, 1),
    (0, 0, -1),
    (1, 1, 0),
    (-1, -1, 0),
    (1, -1, 0),
    (-1, 1, 0),
    (1, 0, 1),
    (-1, 0, -1),
    (1, 0, -1),
    (-1, 0, 1),
    (0, 1, 1),
    (0, -1, -1),
    (0, 1, -1),
    (0, -1, 1),
)
PAD = 8
ROWS = 8
PIECES = 1
ORDER = RISING + FALLING + (0, 3, 4, 5, 6, 15, 16, 17, 18)
PLACE = tuple(ORDER.index(j) for j in range(19))


def moment_table():
    lattice = np.asarray(VELOCITIES, np.float32)
    x, y, z = lattice[:, 0], lattice[:, 1], lattice[:, 2]
    monomials = [np.ones((19,), np.float32), x, y, z, x * y, x * z, y * z, x * x, y * y, z * z]
    monomials += [x * y * y, x * z * z, y * x * x, z * x * x, y * z * z, z * y * y]
    monomials += [x * x * y * y, x * x * z * z, y * y * z * z]
    basis = []
    for vector in monomials:
        for sweep in range(2):
            for earlier in basis:
                vector = vector - np.sum(vector * earlier) * earlier
        basis.append(vector / np.sqrt(np.sum(vector * vector)))
    return np.stack(basis)


TABLE = moment_table()
EVEN_AT = (0, 1, 3, 5, 7, 11, 15)
EVEN_ROWS = (7, 8, 9, 16, 17, 18)
ODD_AT = ((1, 7, 11), (3, 7, 15), (5, 11, 15))
ODD_ROWS = ((10, 11), (12, 14), (13, 15))
MIXED = ((4, 7), (5, 11), (6, 15))


def coefficients(relax_ref):
    def block(at, rows):
        rates = [relax_ref[row] for row in rows]
        out = {}
        for a in range(len(at)):
            for b in range(a, len(at)):
                total = None
                for row, rate in zip(rows, rates):
                    factor = float(TABLE[row, at[a]]) * float(TABLE[row, at[b]])
                    if abs(factor) < 1e-6:
                        continue
                    term = rate * np.float32(factor)
                    total = term if total is None else total + term
                out[a, b] = out[b, a] = total
        return out

    even = block(EVEN_AT, EVEN_ROWS)
    odd = [block(at, rows) for at, rows in zip(ODD_AT, ODD_ROWS)]
    mixed = [relax_ref[row] * np.float32(float(TABLE[row, at]) ** 2) for row, at in MIXED]
    return even, odd, mixed


def apply(block, values):
    result = []
    for a in range(len(values)):
        total = None
        for b, value in enumerate(values):
            if block[a, b] is None:
                continue
            term = block[a, b] * value
            total = term if total is None else total + term
        result.append(total)
    return result


def classes(p):
    even = [p[0], p[1] + p[2], p[3] + p[4], p[5] + p[6]]
    single = [p[1] - p[2], p[3] - p[4], p[5] - p[6]]
    mixed, firsts, seconds = [], [], []
    for base in (7, 11, 15):
        a, b = p[base] + p[base + 1], p[base + 2] + p[base + 3]
        c, d = p[base] - p[base + 1], p[base + 2] - p[base + 3]
        even.append(a + b)
        mixed.append(a - b)
        firsts.append(c + d)
        seconds.append(c - d)
    odd = [
        [single[0], firsts[0], firsts[1]],
        [single[1], seconds[0], firsts[2]],
        [single[2], seconds[1], seconds[2]],
    ]
    return even, odd, mixed


def quadratic(diagonal, mixed, u):
    xx, yy, zz = diagonal
    xy, xz, yz = mixed
    return (
        u[0] * xx + u[1] * xy + u[2] * xz,
        u[0] * xy + u[1] * yy + u[2] * yz,
        u[0] * xz + u[1] * yz + u[2] * zz,
    )


def collide(p, u, fluid, coefs):
    even_block, odd_block, mixed_block = coefs
    even, odd, mixed = classes(p)
    ge = apply(even_block, even)
    go = [apply(block, values) for block, values in zip(odd_block, odd)]
    gm = [scale * value for scale, value in zip(mixed_block, mixed)]
    w0, w1, w2 = np.float32(1 / 3), np.float32(2 / 18), np.float32(4 / 36)
    axes = [w1 * value for value in ge[1:4]]
    planes = [w2 * value for value in ge[4:7]]
    diagonal = (
        axes[0] + (planes[0] + planes[1]),
        axes[1] + (planes[0] + planes[2]),
        axes[2] + (planes[1] + planes[2]),
    )
    total = w0 * ge[0] + (axes[0] + axes[1] + axes[2]) + (planes[0] + planes[1] + planes[2])
    first = [w1 * value[0] + w2 * (value[1] + value[2]) for value in go]
    cross = [w2 * value for value in gm]
    bent = quadratic(diagonal, cross, u)
    speed_sq = u[0] * u[0] + u[1] * u[1] + u[2] * u[2]
    s0 = total * (1.0 + 1.5 * speed_sq) - 4.5 * (u[0] * bent[0] + u[1] * bent[1] + u[2] * bent[2])
    s = [3.0 * (first[i] + 3.0 * bent[i] - u[i] * total) for i in range(3)]
    he = [s0 - value for value in ge]
    ho = [[s[i] - value for value in go[i]] for i in range(3)]
    out = [None] * 19
    out[0] = p[0] + he[0]
    for i in range(3):
        out[1 + 2 * i] = p[1 + 2 * i] + (he[1 + i] + ho[i][0])
        out[2 + 2 * i] = p[2 + 2 * i] + (he[1 + i] - ho[i][0])
    pairs = ((ho[0][1], ho[1][1]), (ho[0][2], ho[2][1]), (ho[1][2], ho[2][2]))
    for i, (left, right) in enumerate(pairs):
        base = 7 + 4 * i
        e, f = he[4 + i] - gm[i], he[4 + i] + gm[i]
        x, y = left + right, left - right
        out[base] = p[base] + (e + x)
        out[base + 1] = p[base + 1] + (e - x)
        out[base + 2] = p[base + 2] + (f + y)
        out[base + 3] = p[base + 3] + (f - y)
    return [jnp.where(fluid, value, 0.0) for value in out]


def wall_value(x, rho, u, fluid):
    even, odd, mixed = classes(x)
    total = sum(even[1:], even[0])
    diagonal = (
        even[1] + (even[4] + even[5]),
        even[2] + (even[4] + even[6]),
        even[3] + (even[5] + even[6]),
    )
    first = [value[0] + (value[1] + value[2]) for value in odd]
    bent = quadratic(diagonal, mixed, u)
    speed_sq = u[0] * u[0] + u[1] * u[1] + u[2] * u[2]
    linear = [3.0 * first[i] + 4.5 * bent[i] for i in range(3)]
    value = total * (1.0 - 1.5 * speed_sq) + (
        u[0] * linear[0] + u[1] * linear[1] + u[2] * linear[2]
    )
    return jnp.where(fluid, rho * value, 0.0)


def split3(value):
    one = value.astype(jnp.bfloat16)
    rest = value - one.astype(jnp.float32)
    two = rest.astype(jnp.bfloat16)
    three = (rest - two.astype(jnp.float32)).astype(jnp.bfloat16)
    return [part.astype(jnp.float32) for part in (one, two, three)]


def one_hot_sums(index, value, low_bits, highs):
    high = lax.shift_right_logical(index, low_bits)
    low = lax.bitwise_and(index, (1 << low_bits) - 1)
    parts = split3(value)
    high_iota = lax.broadcasted_iota(jnp.int32, (highs, 128), 0)
    low_iota = lax.broadcasted_iota(jnp.int32, (128, 128), 0)
    lefts, rights = [], []
    for row in range(ROWS):
        hit = high_iota == high[row : row + 1, :]
        left = [jnp.where(hit, part[row : row + 1, :], 0.0) for part in parts]
        lefts.append(jnp.concatenate(left, axis=0).astype(jnp.bfloat16))
        right = jnp.where(low_iota == low[row : row + 1, :], 1.0, 0.0)
        rights.append(right.astype(jnp.bfloat16))
    return lax.dot_general(
        jnp.concatenate(lefts, axis=1),
        jnp.concatenate(rights, axis=1),
        (((1,), (1,)), ((), ())),
        preferred_element_type=jnp.float32,
    )


def kernel(
    n,
    low_bits,
    relax_hbm,
    adjoint_ref,
    density_ref,
    velocity_ref,
    links_ref,
    patch_ref,
    owner_ref,
    out_ref,
    gradient_ref,
    first,
    second,
    rims_one,
    rims_two,
    rho,
    flow,
    bits,
    patch,
    owner,
    relax_ref,
    wall,
    sums,
    outgoing,
    incoming,
    local_sem,
    send_one,
    recv_one,
    send_two,
    recv_two,
    send_sum,
    recv_sum,
    result,
    out_sem,
    met,
):
    me = lax.axis_index("span")
    above, below = lax.rem(me + 1, n), lax.rem(me + n - 1, n)
    ny = wall.shape[0]
    chunks = ny // ROWS

    def other(d):
        return lax.rem(me + d, n)

    loads = [
        pltpu.make_async_copy(source, target, local_sem.at[i])
        for i, (source, target) in enumerate(
            (
                (adjoint_ref.at[:, 0], first.at[:, pl.ds(PAD, ny), :]),
                (links_ref.at[:, 0], bits),
                (velocity_ref.at[:, :, 0], flow),
                (density_ref.at[:, 0], rho),
                (patch_ref.at[0], patch),
                (owner_ref, owner),
                (relax_hbm, relax_ref),
            )
        )
    ]
    for load in loads:
        load.start()

    barrier = pltpu.get_barrier_semaphore()

    neighbours = (above, below) if n > 2 else (above,)
    for device in neighbours:
        pl.semaphore_signal(barrier, inc=1, device_id={"span": device}, device_id_type=MESH)
    for buffer in (first, second, rims_one, rims_two):
        blank = jnp.zeros((buffer.shape[0], PAD, buffer.shape[2]), jnp.float32)
        buffer[:, 0:PAD, :] = blank
        buffer[:, PAD + ny : PAD + ny + PAD, :] = blank
    pl.semaphore_wait(barrier, len(neighbours))

    pieces = PIECES
    length = ny // pieces
    ends_one = [length * (i + 1) for i in range(pieces)]
    ends_two = [end - ROWS for end in ends_one[:-1]] + [ny]
    ends_out = [end - ROWS for end in ends_two[:-1]] + [ny]

    def send_rims(sources, rims, sems, start, end):
        copies = []
        for i, (slots, source, target) in enumerate(sources(start, end)):
            copies.append(
                pltpu.make_async_remote_copy(
                    src_ref=source,
                    dst_ref=rims.at[slots, pl.ds(PAD + start, end - start), :],
                    send_sem=sems[0].at[i],
                    recv_sem=sems[1].at[i],
                    device_id={"span": target},
                    device_id_type=MESH,
                )
            )
        for copy in copies:
            copy.start()
        return copies

    def sources_one(start, end):
        rows = pl.ds(start, end - start)
        for k in range(5):
            yield k, adjoint_ref.at[RISING[k], 0, rows, :], below
            yield 5 + k, adjoint_ref.at[FALLING[k], 0, rows, :], above

    def sources_two(start, end):
        rows = pl.ds(PAD + start, end - start)
        yield pl.ds(0, 5), second.at[pl.ds(0, 5), rows, :], below
        yield pl.ds(5, 5), second.at[pl.ds(5, 5), rows, :], above

    def meet(i):
        far = 1 << i
        for side, device in enumerate((other(far), other(n - far))):
            pl.semaphore_signal(
                met.at[i, side], inc=1, device_id={"span": device}, device_id_type=MESH
            )

    def met_all(i):
        for side in range(2):
            pl.semaphore_wait(met.at[i, side], 1)

    copies_one = []
    for i, end in enumerate(ends_one):
        sems = (send_one.at[i], recv_one.at[i])
        copies_one.append(send_rims(sources_one, rims_one, sems, end - length, end))
    meet(0)
    for load in loads:
        load.wait()
    coefs = coefficients(relax_ref)

    def masks(rows):
        low, high = bits[0, rows, :], bits[1, rows, :]
        return [
            lax.bitwise_and(low if j < 10 else high, 1 << (j % 10)) != 0 for j in range(19)
        ]

    def walls(level, populations, place, add):
        def step(i, carry):
            start = pl.multiple_of(i * ROWS, ROWS)
            rows = pl.ds(start, ROWS)
            inner = pl.ds(pl.multiple_of(start + PAD, ROWS), ROWS)
            linked = masks(rows)
            u = [flow[level, axis, rows, :] for axis in range(3)]
            x = [
                jnp.where(linked[j], populations[place[OPPOSITE[j]], inner, :], 0.0) for j in range(19)
            ]
            value = wall_value(x, rho[level, rows, :], u, jnp.logical_not(linked[0]))
            wall[rows, :] = wall[rows, :] + value if add else value
            return carry

        lax.fori_loop(0, chunks, step, 0)

    def collisions(level, populations, place, rims, store, begin, end):
        def step(i, carry):
            start = pl.multiple_of(i * ROWS, ROWS)
            rows = pl.ds(start, ROWS)
            inner = pl.ds(pl.multiple_of(start + PAD, ROWS), ROWS)
            linked = masks(rows)
            u = [flow[level, axis, rows, :] for axis in range(3)]
            p = []
            for j, (step_x, step_y, step_z) in enumerate(VELOCITIES):
                shifted = inner if step_y == 0 else pl.ds(start + (PAD + step_y), ROWS)
                if step_x == 1:
                    upstream = rims[RISING.index(j), shifted, :]
                elif step_x == -1:
                    upstream = rims[5 + FALLING.index(j), shifted, :]
                else:
                    upstream = populations[place[j], shifted, :]
                if step_z != 0:
                    upstream = pltpu.roll(upstream, (-step_z) % upstream.shape[1], 1)
                p.append(jnp.where(linked[j], populations[place[OPPOSITE[j]], inner, :], upstream))
            for j, value in enumerate(collide(p, u, jnp.logical_not(linked[0]), coefs)):
                store(j, rows, inner, value)
            return carry

        lax.fori_loop(begin // ROWS, end // ROWS, step, 0)

    def store_second(j, rows, inner, value):
        second[PLACE[j], inner, :] = value

    walls(1, first, range(19), False)
    rounds = met.shape[0]
    for i in range(rounds):
        met_all(i)
        if i + 1 < rounds:
            meet(i + 1)
    copies_two = []
    for i, end in enumerate(ends_two):
        for copy in copies_one[i]:
            copy.wait_recv()
        start = ends_two[i - 1] if i else 0
        collisions(1, first, range(19), rims_one, store_second, start, end)
        sems = (send_two.at[i], recv_two.at[i])
        copies_two.append(send_rims(sources_two, rims_two, sems, start, end))

    walls(0, second, PLACE, True)

    def by_patch(i, total):
        rows = pl.ds(pl.multiple_of(i * ROWS, ROWS), ROWS)
        return total + one_hot_sums(patch[rows, :], wall[rows, :], 7, owner.shape[0])

    highs = owner.shape[0]
    total = lax.fori_loop(0, chunks, by_patch, jnp.zeros((3 * highs, 128), jnp.float32))
    sums[...] = total[:highs] + (total[highs : 2 * highs] + total[2 * highs :])

    targets = outgoing.shape[0] * outgoing.shape[1]

    def by_owner(i, total):
        rows = pl.ds(pl.multiple_of(i * ROWS, ROWS), ROWS)
        return total + one_hot_sums(owner[rows, :], sums[rows, :], low_bits, targets)

    total = lax.fori_loop(
        0, highs // ROWS, by_owner, jnp.zeros((3 * targets, 128), jnp.float32)
    )
    placed = total[:targets] + (total[targets : 2 * targets] + total[2 * targets :])
    per = outgoing.shape[1]
    for i in range(n):
        outgoing[i] = placed[i * per : (i + 1) * per]

    def sum_copy(d, source):
        return pltpu.make_async_remote_copy(
            src_ref=outgoing.at[other(d)],
            dst_ref=incoming.at[source],
            send_sem=send_sum.at[d],
            recv_sem=recv_sum.at[source],
            device_id={"span": other(d)},
            device_id_type=MESH,
        )

    def send(d, carry):
        sum_copy(d, me).start()
        return carry

    lax.fori_loop(1, n, send, 0)

    def store_out(j, rows, inner, value):
        result[j, 0, rows, :] = value

    out_copies = []
    for i, end in enumerate(ends_out):
        for copy in copies_two[i]:
            copy.wait_recv()
        start = ends_out[i - 1] if i else 0
        collisions(0, second, PLACE, rims_two, store_out, start, end)
        rows = pl.ds(start, end - start)
        out_copies.append(
            pltpu.make_async_copy(
                result.at[:, :, rows, :], out_ref.at[:, :, rows, :], out_sem.at[i]
            )
        )
        out_copies[-1].start()

    def collect(d, total):
        source = other(n - d)
        sum_copy(d, source).wait_recv()
        return total + incoming[source]

    gradient_ref[...] = lax.fori_loop(1, n, collect, outgoing[me])

    def sent(d, carry):
        sum_copy(d, me).wait_send()
        return carry

    lax.fori_loop(1, n, sent, 0)
    for copies in copies_one + copies_two:
        for copy in copies:
            copy.wait_send()
    for copy in out_copies:
        copy.wait()


def body(n, adjoint_in, density, velocity, links, patch_map, owner, relax):
    _, planes, ny, nz = adjoint_in.shape
    assert planes == 1 and nz == 128 and ny % ROWS == 0
    rows = owner.shape[0] // n
    low = min(128, rows)
    per = rows // low
    highs = owner.shape[0] // 128
    padded = ny + 2 * PAD
    hbm = pl.BlockSpec(memory_space=pltpu.HBM)
    vmem = pl.BlockSpec(memory_space=pltpu.VMEM)
    levels = density.shape[0]
    rounds = max(1, (n // 2 - 1).bit_length())
    adjoint, gradient = pl.pallas_call(
        functools.partial(kernel, n, low.bit_length() - 1),
        out_shape=(
            jax.ShapeDtypeStruct(adjoint_in.shape, jnp.float32),
            jax.ShapeDtypeStruct((per, 128), jnp.float32),
        ),
        in_specs=[hbm] * 7,
        out_specs=(hbm, vmem),
        scratch_shapes=[
            pltpu.VMEM((19, padded, nz), jnp.float32),
            pltpu.VMEM((19, padded, nz), jnp.float32),
            pltpu.VMEM((10, padded, nz), jnp.float32),
            pltpu.VMEM((10, padded, nz), jnp.float32),
            pltpu.VMEM((levels, ny, nz), jnp.float32),
            pltpu.VMEM((levels, 3, ny, nz), jnp.float32),
            pltpu.VMEM((2, ny, nz), jnp.int32),
            pltpu.VMEM((ny, nz), jnp.int32),
            pltpu.VMEM((highs, 128), jnp.int32),
            pltpu.SMEM(relax.shape, jnp.float32),
            pltpu.VMEM((ny, nz), jnp.float32),
            pltpu.VMEM((highs, 128), jnp.float32),
            pltpu.VMEM((n, per, 128), jnp.float32),
            pltpu.VMEM((n, per, 128), jnp.float32),
            pltpu.SemaphoreType.DMA((7,)),
            pltpu.SemaphoreType.DMA((PIECES, 10)),
            pltpu.SemaphoreType.DMA((PIECES, 10)),
            pltpu.SemaphoreType.DMA((PIECES, 2)),
            pltpu.SemaphoreType.DMA((PIECES, 2)),
            pltpu.SemaphoreType.DMA((n,)),
            pltpu.SemaphoreType.DMA((n,)),
            pltpu.VMEM(adjoint_in.shape, jnp.float32),
            pltpu.SemaphoreType.DMA((PIECES,)),
            pltpu.SemaphoreType.REGULAR((rounds, 2)),
        ],
        compiler_params=pltpu.CompilerParams(
            collective_id=0, has_side_effects=True, vmem_limit_bytes=60 * 1024 * 1024
        ),
        cost_estimate=pl.CostEstimate(
            flops=40_000_000, bytes_accessed=4_000_000, transcendentals=0
        ),
    )(relax, adjoint_in, density, velocity, links, patch_map, owner.reshape(highs, 128))
    return adjoint, gradient[:, :low].reshape(rows)


def solution(mesh):
    in_specs = (
        P("case", "span", None, None),
        P("case", "span", None, None),
        P("case", None, "span", None, None),
        P(None, ("case", "span"), None, None),
        P(("case", "span"), None, None),
        P(),
        P("case"),
    )
    out_specs = (P("case", "span", None, None), P(("case", "span")))
    return jax.shard_map(
        functools.partial(body, mesh.shape["span"]),
        mesh=mesh,
        in_specs=in_specs,
        out_specs=out_specs,
        check_vma=False,
    )
```

```python
import functools

import jax
import jax.numpy as jnp
import numpy as np
from jax import lax
from jax.experimental import pallas as pl
from jax.experimental.pallas import tpu as pltpu
from jax.sharding import PartitionSpec as P

MESH = pl.DeviceIdType.MESH
RISING = (1, 7, 9, 11, 13)
FALLING = (2, 8, 10, 12, 14)
OPPOSITE = (0, 2, 1, 4, 3, 6, 5, 8, 7, 10, 9, 12, 11, 14, 13, 16, 15, 18, 17)
VELOCITIES = (
    (0, 0, 0),
    (1, 0, 0),
    (-1, 0, 0),
    (0, 1, 0),
    (0, -1, 0),
    (0, 0, 1),
    (0, 0, -1),
    (1, 1, 0),
    (-1, -1, 0),
    (1, -1, 0),
    (-1, 1, 0),
    (1, 0, 1),
    (-1, 0, -1),
    (1, 0, -1),
    (-1, 0, 1),
    (0, 1, 1),
    (0, -1, -1),
    (0, 1, -1),
    (0, -1, 1),
)
PAD = 8
ROWS = 8
PIECES = 1
ORDER = RISING + FALLING + (0, 3, 4, 5, 6, 15, 16, 17, 18)
PLACE = tuple(ORDER.index(j) for j in range(19))


def moment_table():
    lattice = np.asarray(VELOCITIES, np.float32)
    x, y, z = lattice[:, 0], lattice[:, 1], lattice[:, 2]
    monomials = [np.ones((19,), np.float32), x, y, z, x * y, x * z, y * z, x * x, y * y, z * z]
    monomials += [x * y * y, x * z * z, y * x * x, z * x * x, y * z * z, z * y * y]
    monomials += [x * x * y * y, x * x * z * z, y * y * z * z]
    basis = []
    for vector in monomials:
        for sweep in range(2):
            for earlier in basis:
                vector = vector - np.sum(vector * earlier) * earlier
        basis.append(vector / np.sqrt(np.sum(vector * vector)))
    return np.stack(basis)


TABLE = moment_table()
EVEN_AT = (0, 1, 3, 5, 7, 11, 15)
EVEN_ROWS = (7, 8, 9, 16, 17, 18)
ODD_AT = ((1, 7, 11), (3, 7, 15), (5, 11, 15))
ODD_ROWS = ((10, 11), (12, 14), (13, 15))
MIXED = ((4, 7), (5, 11), (6, 15))


def coefficients(relax_ref):
    def block(at, rows):
        rates = [relax_ref[row] for row in rows]
        out = {}
        for a in range(len(at)):
            for b in range(a, len(at)):
                total = None
                for row, rate in zip(rows, rates):
                    factor = float(TABLE[row, at[a]]) * float(TABLE[row, at[b]])
                    if abs(factor) < 1e-6:
                        continue
                    term = rate * np.float32(factor)
                    total = term if total is None else total + term
                out[a, b] = out[b, a] = total
        return out

    even = block(EVEN_AT, EVEN_ROWS)
    odd = [block(at, rows) for at, rows in zip(ODD_AT, ODD_ROWS)]
    mixed = [relax_ref[row] * np.float32(float(TABLE[row, at]) ** 2) for row, at in MIXED]
    return even, odd, mixed


def apply(block, values):
    result = []
    for a in range(len(values)):
        total = None
        for b, value in enumerate(values):
            if block[a, b] is None:
                continue
            term = block[a, b] * value
            total = term if total is None else total + term
        result.append(total)
    return result


def classes(p):
    even = [p[0], p[1] + p[2], p[3] + p[4], p[5] + p[6]]
    single = [p[1] - p[2], p[3] - p[4], p[5] - p[6]]
    mixed, firsts, seconds = [], [], []
    for base in (7, 11, 15):
        a, b = p[base] + p[base + 1], p[base + 2] + p[base + 3]
        c, d = p[base] - p[base + 1], p[base + 2] - p[base + 3]
        even.append(a + b)
        mixed.append(a - b)
        firsts.append(c + d)
        seconds.append(c - d)
    odd = [
        [single[0], firsts[0], firsts[1]],
        [single[1], seconds[0], firsts[2]],
        [single[2], seconds[1], seconds[2]],
    ]
    return even, odd, mixed


def quadratic(diagonal, mixed, u):
    xx, yy, zz = diagonal
    xy, xz, yz = mixed
    return (
        u[0] * xx + u[1] * xy + u[2] * xz,
        u[0] * xy + u[1] * yy + u[2] * yz,
        u[0] * xz + u[1] * yz + u[2] * zz,
    )


def collide(p, u, fluid, coefs):
    even_block, odd_block, mixed_block = coefs
    even, odd, mixed = classes(p)
    ge = apply(even_block, even)
    go = [apply(block, values) for block, values in zip(odd_block, odd)]
    gm = [scale * value for scale, value in zip(mixed_block, mixed)]
    w0, w1, w2 = np.float32(1 / 3), np.float32(2 / 18), np.float32(4 / 36)
    axes = [w1 * value for value in ge[1:4]]
    planes = [w2 * value for value in ge[4:7]]
    diagonal = (
        axes[0] + (planes[0] + planes[1]),
        axes[1] + (planes[0] + planes[2]),
        axes[2] + (planes[1] + planes[2]),
    )
    total = w0 * ge[0] + (axes[0] + axes[1] + axes[2]) + (planes[0] + planes[1] + planes[2])
    first = [w1 * value[0] + w2 * (value[1] + value[2]) for value in go]
    cross = [w2 * value for value in gm]
    bent = quadratic(diagonal, cross, u)
    speed_sq = u[0] * u[0] + u[1] * u[1] + u[2] * u[2]
    s0 = total * (1.0 + 1.5 * speed_sq) - 4.5 * (u[0] * bent[0] + u[1] * bent[1] + u[2] * bent[2])
    s = [3.0 * (first[i] + 3.0 * bent[i] - u[i] * total) for i in range(3)]
    he = [s0 - value for value in ge]
    ho = [[s[i] - value for value in go[i]] for i in range(3)]
    out = [None] * 19
    out[0] = p[0] + he[0]
    for i in range(3):
        out[1 + 2 * i] = p[1 + 2 * i] + (he[1 + i] + ho[i][0])
        out[2 + 2 * i] = p[2 + 2 * i] + (he[1 + i] - ho[i][0])
    pairs = ((ho[0][1], ho[1][1]), (ho[0][2], ho[2][1]), (ho[1][2], ho[2][2]))
    for i, (left, right) in enumerate(pairs):
        base = 7 + 4 * i
        e, f = he[4 + i] - gm[i], he[4 + i] + gm[i]
        x, y = left + right, left - right
        out[base] = p[base] + (e + x)
        out[base + 1] = p[base + 1] + (e - x)
        out[base + 2] = p[base + 2] + (f + y)
        out[base + 3] = p[base + 3] + (f - y)
    return [jnp.where(fluid, value, 0.0) for value in out]


def wall_value(x, rho, u, fluid):
    even, odd, mixed = classes(x)
    total = sum(even[1:], even[0])
    diagonal = (
        even[1] + (even[4] + even[5]),
        even[2] + (even[4] + even[6]),
        even[3] + (even[5] + even[6]),
    )
    first = [value[0] + (value[1] + value[2]) for value in odd]
    bent = quadratic(diagonal, mixed, u)
    speed_sq = u[0] * u[0] + u[1] * u[1] + u[2] * u[2]
    linear = [3.0 * first[i] + 4.5 * bent[i] for i in range(3)]
    value = total * (1.0 - 1.5 * speed_sq) + (
        u[0] * linear[0] + u[1] * linear[1] + u[2] * linear[2]
    )
    return jnp.where(fluid, rho * value, 0.0)


def split3(value):
    one = value.astype(jnp.bfloat16)
    rest = value - one.astype(jnp.float32)
    two = rest.astype(jnp.bfloat16)
    three = (rest - two.astype(jnp.float32)).astype(jnp.bfloat16)
    return [part.astype(jnp.float32) for part in (one, two, three)]


def one_hot_sums(index, value, low_bits, highs):
    high = lax.shift_right_logical(index, low_bits)
    low = lax.bitwise_and(index, (1 << low_bits) - 1)
    parts = split3(value)
    high_iota = lax.broadcasted_iota(jnp.int32, (highs, 128), 0)
    low_iota = lax.broadcasted_iota(jnp.int32, (128, 128), 0)
    lefts, rights = [], []
    for row in range(ROWS):
        hit = high_iota == high[row : row + 1, :]
        left = [jnp.where(hit, part[row : row + 1, :], 0.0) for part in parts]
        lefts.append(jnp.concatenate(left, axis=0).astype(jnp.bfloat16))
        right = jnp.where(low_iota == low[row : row + 1, :], 1.0, 0.0)
        rights.append(right.astype(jnp.bfloat16))
    return lax.dot_general(
        jnp.concatenate(lefts, axis=1),
        jnp.concatenate(rights, axis=1),
        (((1,), (1,)), ((), ())),
        preferred_element_type=jnp.float32,
    )


def kernel(
    n,
    low_bits,
    relax_hbm,
    adjoint_ref,
    density_ref,
    velocity_ref,
    links_ref,
    patch_ref,
    owner_ref,
    out_ref,
    gradient_ref,
    first,
    second,
    rims_one,
    rims_two,
    rho,
    flow,
    bits,
    patch,
    owner,
    relax_ref,
    wall,
    sums,
    outgoing,
    incoming,
    local_sem,
    send_one,
    recv_one,
    send_two,
    recv_two,
    send_sum,
    recv_sum,
    met,
):
    me = lax.axis_index("span")
    above, below = lax.rem(me + 1, n), lax.rem(me + n - 1, n)
    ny = wall.shape[0]
    chunks = ny // ROWS

    def other(d):
        return lax.rem(me + d, n)

    loads = [
        pltpu.make_async_copy(source, target, local_sem.at[i])
        for i, (source, target) in enumerate(
            (
                (adjoint_ref.at[:, 0], first.at[:, pl.ds(PAD, ny), :]),
                (links_ref.at[:, 0], bits),
                (velocity_ref.at[:, :, 0], flow),
                (density_ref.at[:, 0], rho),
                (patch_ref.at[0], patch),
                (owner_ref, owner),
                (relax_hbm, relax_ref),
            )
        )
    ]
    for load in loads:
        load.start()

    barrier = pltpu.get_barrier_semaphore()

    neighbours = (above, below) if n > 2 else (above,)
    for device in neighbours:
        pl.semaphore_signal(barrier, inc=1, device_id={"span": device}, device_id_type=MESH)
    for buffer in (first, second, rims_one, rims_two):
        blank = jnp.zeros((buffer.shape[0], PAD, buffer.shape[2]), jnp.float32)
        buffer[:, 0:PAD, :] = blank
        buffer[:, PAD + ny : PAD + ny + PAD, :] = blank
    pl.semaphore_wait(barrier, len(neighbours))

    pieces = PIECES
    length = ny // pieces
    ends_one = [length * (i + 1) for i in range(pieces)]
    ends_two = [end - ROWS for end in ends_one[:-1]] + [ny]
    ends_out = [end - ROWS for end in ends_two[:-1]] + [ny]

    def send_rims(sources, rims, sems, start, end):
        copies = []
        for i, (slots, source, target) in enumerate(sources(start, end)):
            copies.append(
                pltpu.make_async_remote_copy(
                    src_ref=source,
                    dst_ref=rims.at[slots, pl.ds(PAD + start, end - start), :],
                    send_sem=sems[0].at[i],
                    recv_sem=sems[1].at[i],
                    device_id={"span": target},
                    device_id_type=MESH,
                )
            )
        for copy in copies:
            copy.start()
        return copies

    def sources_one(start, end):
        rows = pl.ds(start, end - start)
        for k in range(5):
            yield k, adjoint_ref.at[RISING[k], 0, rows, :], below
            yield 5 + k, adjoint_ref.at[FALLING[k], 0, rows, :], above

    def sources_two(start, end):
        rows = pl.ds(PAD + start, end - start)
        yield pl.ds(0, 5), second.at[pl.ds(0, 5), rows, :], below
        yield pl.ds(5, 5), second.at[pl.ds(5, 5), rows, :], above

    def meet(i):
        far = 1 << i
        for side, device in enumerate((other(far), other(n - far))):
            pl.semaphore_signal(
                met.at[i, side], inc=1, device_id={"span": device}, device_id_type=MESH
            )

    def met_all(i):
        for side in range(2):
            pl.semaphore_wait(met.at[i, side], 1)

    copies_one = []
    for i, end in enumerate(ends_one):
        sems = (send_one.at[i], recv_one.at[i])
        copies_one.append(send_rims(sources_one, rims_one, sems, end - length, end))
    meet(0)
    for load in loads:
        load.wait()
    coefs = coefficients(relax_ref)

    def masks(rows):
        low, high = bits[0, rows, :], bits[1, rows, :]
        return [
            lax.bitwise_and(low if j < 10 else high, 1 << (j % 10)) != 0 for j in range(19)
        ]

    def walls(level, populations, place, add):
        def step(i, carry):
            start = pl.multiple_of(i * ROWS, ROWS)
            rows = pl.ds(start, ROWS)
            inner = pl.ds(pl.multiple_of(start + PAD, ROWS), ROWS)
            linked = masks(rows)
            u = [flow[level, axis, rows, :] for axis in range(3)]
            x = [
                jnp.where(linked[j], populations[place[OPPOSITE[j]], inner, :], 0.0) for j in range(19)
            ]
            value = wall_value(x, rho[level, rows, :], u, jnp.logical_not(linked[0]))
            wall[rows, :] = wall[rows, :] + value if add else value
            return carry

        lax.fori_loop(0, chunks, step, 0)

    def collisions(level, populations, place, rims, store, begin, end):
        def step(i, carry):
            start = pl.multiple_of(i * ROWS, ROWS)
            rows = pl.ds(start, ROWS)
            inner = pl.ds(pl.multiple_of(start + PAD, ROWS), ROWS)
            linked = masks(rows)
            u = [flow[level, axis, rows, :] for axis in range(3)]
            p = []
            for j, (step_x, step_y, step_z) in enumerate(VELOCITIES):
                shifted = inner if step_y == 0 else pl.ds(start + (PAD + step_y), ROWS)
                if step_x == 1:
                    upstream = rims[RISING.index(j), shifted, :]
                elif step_x == -1:
                    upstream = rims[5 + FALLING.index(j), shifted, :]
                else:
                    upstream = populations[place[j], shifted, :]
                if step_z != 0:
                    upstream = pltpu.roll(upstream, (-step_z) % upstream.shape[1], 1)
                p.append(jnp.where(linked[j], populations[place[OPPOSITE[j]], inner, :], upstream))
            for j, value in enumerate(collide(p, u, jnp.logical_not(linked[0]), coefs)):
                store(j, rows, inner, value)
            return carry

        lax.fori_loop(begin // ROWS, end // ROWS, step, 0)

    def store_second(j, rows, inner, value):
        second[PLACE[j], inner, :] = value

    walls(1, first, range(19), False)
    rounds = met.shape[0]
    for i in range(rounds):
        met_all(i)
        if i + 1 < rounds:
            meet(i + 1)
    copies_two = []
    for i, end in enumerate(ends_two):
        for copy in copies_one[i]:
            copy.wait_recv()
        start = ends_two[i - 1] if i else 0
        collisions(1, first, range(19), rims_one, store_second, start, end)
        sems = (send_two.at[i], recv_two.at[i])
        copies_two.append(send_rims(sources_two, rims_two, sems, start, end))

    walls(0, second, PLACE, True)

    def by_patch(i, total):
        rows = pl.ds(pl.multiple_of(i * ROWS, ROWS), ROWS)
        return total + one_hot_sums(patch[rows, :], wall[rows, :], 7, owner.shape[0])

    highs = owner.shape[0]
    total = lax.fori_loop(0, chunks, by_patch, jnp.zeros((3 * highs, 128), jnp.float32))
    sums[...] = total[:highs] + (total[highs : 2 * highs] + total[2 * highs :])

    targets = outgoing.shape[0] * outgoing.shape[1]

    def by_owner(i, total):
        rows = pl.ds(pl.multiple_of(i * ROWS, ROWS), ROWS)
        return total + one_hot_sums(owner[rows, :], sums[rows, :], low_bits, targets)

    total = lax.fori_loop(
        0, highs // ROWS, by_owner, jnp.zeros((3 * targets, 128), jnp.float32)
    )
    placed = total[:targets] + (total[targets : 2 * targets] + total[2 * targets :])
    per = outgoing.shape[1]
    for i in range(n):
        outgoing[i] = placed[i * per : (i + 1) * per]

    def sum_copy(d, source):
        return pltpu.make_async_remote_copy(
            src_ref=outgoing.at[other(d)],
            dst_ref=incoming.at[source],
            send_sem=send_sum.at[d],
            recv_sem=recv_sum.at[source],
            device_id={"span": other(d)},
            device_id_type=MESH,
        )

    def send(d, carry):
        sum_copy(d, me).start()
        return carry

    lax.fori_loop(1, n, send, 0)

    def store_out(j, rows, inner, value):
        out_ref[j, 0, rows, :] = value

    for i, end in enumerate(ends_out):
        for copy in copies_two[i]:
            copy.wait_recv()
        start = ends_out[i - 1] if i else 0
        collisions(0, second, PLACE, rims_two, store_out, start, end)

    def collect(d, total):
        source = other(n - d)
        sum_copy(d, source).wait_recv()
        return total + incoming[source]

    gradient_ref[...] = lax.fori_loop(1, n, collect, outgoing[me])

    def sent(d, carry):
        sum_copy(d, me).wait_send()
        return carry

    lax.fori_loop(1, n, sent, 0)
    for copies in copies_one + copies_two:
        for copy in copies:
            copy.wait_send()


def body(n, adjoint_in, density, velocity, links, patch_map, owner, relax):
    _, planes, ny, nz = adjoint_in.shape
    assert planes == 1 and nz == 128 and ny % ROWS == 0
    rows = owner.shape[0] // n
    low = min(128, rows)
    per = rows // low
    highs = owner.shape[0] // 128
    padded = ny + 2 * PAD
    hbm = pl.BlockSpec(memory_space=pltpu.HBM)
    vmem = pl.BlockSpec(memory_space=pltpu.VMEM)
    levels = density.shape[0]
    rounds = max(1, (n // 2 - 1).bit_length())
    adjoint, gradient = pl.pallas_call(
        functools.partial(kernel, n, low.bit_length() - 1),
        out_shape=(
            pltpu.VMEM(adjoint_in.shape, jnp.float32),
            pltpu.VMEM((per, 128), jnp.float32),
        ),
        in_specs=[hbm] * 7,
        out_specs=(vmem, vmem),
        scratch_shapes=[
            pltpu.VMEM((19, padded, nz), jnp.float32),
            pltpu.VMEM((19, padded, nz), jnp.float32),
            pltpu.VMEM((10, padded, nz), jnp.float32),
            pltpu.VMEM((10, padded, nz), jnp.float32),
            pltpu.VMEM((levels, ny, nz), jnp.float32),
            pltpu.VMEM((levels, 3, ny, nz), jnp.float32),
            pltpu.VMEM((2, ny, nz), jnp.int32),
            pltpu.VMEM((ny, nz), jnp.int32),
            pltpu.VMEM((highs, 128), jnp.int32),
            pltpu.SMEM(relax.shape, jnp.float32),
            pltpu.VMEM((ny, nz), jnp.float32),
            pltpu.VMEM((highs, 128), jnp.float32),
            pltpu.VMEM((n, per, 128), jnp.float32),
            pltpu.VMEM((n, per, 128), jnp.float32),
            pltpu.SemaphoreType.DMA((7,)),
            pltpu.SemaphoreType.DMA((PIECES, 10)),
            pltpu.SemaphoreType.DMA((PIECES, 10)),
            pltpu.SemaphoreType.DMA((PIECES, 2)),
            pltpu.SemaphoreType.DMA((PIECES, 2)),
            pltpu.SemaphoreType.DMA((n,)),
            pltpu.SemaphoreType.DMA((n,)),
            pltpu.SemaphoreType.REGULAR((rounds, 2)),
        ],
        compiler_params=pltpu.CompilerParams(
            collective_id=0, has_side_effects=True, vmem_limit_bytes=60 * 1024 * 1024
        ),
        cost_estimate=pl.CostEstimate(
            flops=40_000_000, bytes_accessed=4_000_000, transcendentals=0
        ),
    )(relax, adjoint_in, density, velocity, links, patch_map, owner.reshape(highs, 128))
    return adjoint, gradient[:, :low].reshape(rows)


def solution(mesh):
    in_specs = (
        P("case", "span", None, None),
        P("case", "span", None, None),
        P("case", None, "span", None, None),
        P(None, ("case", "span"), None, None),
        P(("case", "span"), None, None),
        P(),
        P("case"),
    )
    out_specs = (P("case", "span", None, None), P(("case", "span")))
    return jax.shard_map(
        functools.partial(body, mesh.shape["span"]),
        mesh=mesh,
        in_specs=in_specs,
        out_specs=out_specs,
        check_vma=False,
    )
```

```python
import functools

import jax
import jax.numpy as jnp
import numpy as np
from jax import lax
from jax.experimental import pallas as pl
from jax.experimental.pallas import tpu as pltpu
from jax.sharding import PartitionSpec as P

MESH = pl.DeviceIdType.MESH
RISING = (1, 7, 9, 11, 13)
FALLING = (2, 8, 10, 12, 14)
OPPOSITE = (0, 2, 1, 4, 3, 6, 5, 8, 7, 10, 9, 12, 11, 14, 13, 16, 15, 18, 17)
VELOCITIES = (
    (0, 0, 0),
    (1, 0, 0),
    (-1, 0, 0),
    (0, 1, 0),
    (0, -1, 0),
    (0, 0, 1),
    (0, 0, -1),
    (1, 1, 0),
    (-1, -1, 0),
    (1, -1, 0),
    (-1, 1, 0),
    (1, 0, 1),
    (-1, 0, -1),
    (1, 0, -1),
    (-1, 0, 1),
    (0, 1, 1),
    (0, -1, -1),
    (0, 1, -1),
    (0, -1, 1),
)
PAD = 8
ROWS = 8
PIECES = 1
ORDER = RISING + FALLING + (0, 3, 4, 5, 6, 15, 16, 17, 18)
PLACE = tuple(ORDER.index(j) for j in range(19))


def moment_table():
    lattice = np.asarray(VELOCITIES, np.float32)
    x, y, z = lattice[:, 0], lattice[:, 1], lattice[:, 2]
    monomials = [np.ones((19,), np.float32), x, y, z, x * y, x * z, y * z, x * x, y * y, z * z]
    monomials += [x * y * y, x * z * z, y * x * x, z * x * x, y * z * z, z * y * y]
    monomials += [x * x * y * y, x * x * z * z, y * y * z * z]
    basis = []
    for vector in monomials:
        for sweep in range(2):
            for earlier in basis:
                vector = vector - np.sum(vector * earlier) * earlier
        basis.append(vector / np.sqrt(np.sum(vector * vector)))
    return np.stack(basis)


TABLE = moment_table()
EVEN_AT = (0, 1, 3, 5, 7, 11, 15)
EVEN_ROWS = (7, 8, 9, 16, 17, 18)
ODD_AT = ((1, 7, 11), (3, 7, 15), (5, 11, 15))
ODD_ROWS = ((10, 11), (12, 14), (13, 15))
MIXED = ((4, 7), (5, 11), (6, 15))


def coefficients(relax_ref):
    def block(at, rows):
        rates = [relax_ref[row] for row in rows]
        out = {}
        for a in range(len(at)):
            for b in range(a, len(at)):
                total = None
                for row, rate in zip(rows, rates):
                    factor = float(TABLE[row, at[a]]) * float(TABLE[row, at[b]])
                    if abs(factor) < 1e-6:
                        continue
                    term = rate * np.float32(factor)
                    total = term if total is None else total + term
                out[a, b] = out[b, a] = total
        return out

    even = block(EVEN_AT, EVEN_ROWS)
    odd = [block(at, rows) for at, rows in zip(ODD_AT, ODD_ROWS)]
    mixed = [relax_ref[row] * np.float32(float(TABLE[row, at]) ** 2) for row, at in MIXED]
    return even, odd, mixed


def apply(block, values):
    result = []
    for a in range(len(values)):
        total = None
        for b, value in enumerate(values):
            if block[a, b] is None:
                continue
            term = block[a, b] * value
            total = term if total is None else total + term
        result.append(total)
    return result


def classes(p):
    even = [p[0], p[1] + p[2], p[3] + p[4], p[5] + p[6]]
    single = [p[1] - p[2], p[3] - p[4], p[5] - p[6]]
    mixed, firsts, seconds = [], [], []
    for base in (7, 11, 15):
        a, b = p[base] + p[base + 1], p[base + 2] + p[base + 3]
        c, d = p[base] - p[base + 1], p[base + 2] - p[base + 3]
        even.append(a + b)
        mixed.append(a - b)
        firsts.append(c + d)
        seconds.append(c - d)
    odd = [
        [single[0], firsts[0], firsts[1]],
        [single[1], seconds[0], firsts[2]],
        [single[2], seconds[1], seconds[2]],
    ]
    return even, odd, mixed


def quadratic(diagonal, mixed, u):
    xx, yy, zz = diagonal
    xy, xz, yz = mixed
    return (
        u[0] * xx + u[1] * xy + u[2] * xz,
        u[0] * xy + u[1] * yy + u[2] * yz,
        u[0] * xz + u[1] * yz + u[2] * zz,
    )


def collide(p, u, fluid, coefs):
    even_block, odd_block, mixed_block = coefs
    even, odd, mixed = classes(p)
    ge = apply(even_block, even)
    go = [apply(block, values) for block, values in zip(odd_block, odd)]
    gm = [scale * value for scale, value in zip(mixed_block, mixed)]
    w0, w1, w2 = np.float32(1 / 3), np.float32(2 / 18), np.float32(4 / 36)
    axes = [w1 * value for value in ge[1:4]]
    planes = [w2 * value for value in ge[4:7]]
    diagonal = (
        axes[0] + (planes[0] + planes[1]),
        axes[1] + (planes[0] + planes[2]),
        axes[2] + (planes[1] + planes[2]),
    )
    total = w0 * ge[0] + (axes[0] + axes[1] + axes[2]) + (planes[0] + planes[1] + planes[2])
    first = [w1 * value[0] + w2 * (value[1] + value[2]) for value in go]
    cross = [w2 * value for value in gm]
    bent = quadratic(diagonal, cross, u)
    speed_sq = u[0] * u[0] + u[1] * u[1] + u[2] * u[2]
    s0 = total * (1.0 + 1.5 * speed_sq) - 4.5 * (u[0] * bent[0] + u[1] * bent[1] + u[2] * bent[2])
    s = [3.0 * (first[i] + 3.0 * bent[i] - u[i] * total) for i in range(3)]
    he = [s0 - value for value in ge]
    ho = [[s[i] - value for value in go[i]] for i in range(3)]
    out = [None] * 19
    out[0] = p[0] + he[0]
    for i in range(3):
        out[1 + 2 * i] = p[1 + 2 * i] + (he[1 + i] + ho[i][0])
        out[2 + 2 * i] = p[2 + 2 * i] + (he[1 + i] - ho[i][0])
    pairs = ((ho[0][1], ho[1][1]), (ho[0][2], ho[2][1]), (ho[1][2], ho[2][2]))
    for i, (left, right) in enumerate(pairs):
        base = 7 + 4 * i
        e, f = he[4 + i] - gm[i], he[4 + i] + gm[i]
        x, y = left + right, left - right
        out[base] = p[base] + (e + x)
        out[base + 1] = p[base + 1] + (e - x)
        out[base + 2] = p[base + 2] + (f + y)
        out[base + 3] = p[base + 3] + (f - y)
    return [jnp.where(fluid, value, 0.0) for value in out]


def wall_value(x, rho, u, fluid):
    even, odd, mixed = classes(x)
    total = sum(even[1:], even[0])
    diagonal = (
        even[1] + (even[4] + even[5]),
        even[2] + (even[4] + even[6]),
        even[3] + (even[5] + even[6]),
    )
    first = [value[0] + (value[1] + value[2]) for value in odd]
    bent = quadratic(diagonal, mixed, u)
    speed_sq = u[0] * u[0] + u[1] * u[1] + u[2] * u[2]
    linear = [3.0 * first[i] + 4.5 * bent[i] for i in range(3)]
    value = total * (1.0 - 1.5 * speed_sq) + (
        u[0] * linear[0] + u[1] * linear[1] + u[2] * linear[2]
    )
    return jnp.where(fluid, rho * value, 0.0)


def split3(value):
    one = value.astype(jnp.bfloat16)
    rest = value - one.astype(jnp.float32)
    two = rest.astype(jnp.bfloat16)
    three = (rest - two.astype(jnp.float32)).astype(jnp.bfloat16)
    return [part.astype(jnp.float32) for part in (one, two, three)]


def one_hot_sums(index, value, low_bits, highs):
    high = lax.shift_right_logical(index, low_bits)
    low = lax.bitwise_and(index, (1 << low_bits) - 1)
    parts = split3(value)
    high_iota = lax.broadcasted_iota(jnp.int32, (highs, 128), 0)
    low_iota = lax.broadcasted_iota(jnp.int32, (128, 128), 0)
    lefts, rights = [], []
    for row in range(ROWS):
        hit = high_iota == high[row : row + 1, :]
        left = [jnp.where(hit, part[row : row + 1, :], 0.0) for part in parts]
        lefts.append(jnp.concatenate(left, axis=0).astype(jnp.bfloat16))
        right = jnp.where(low_iota == low[row : row + 1, :], 1.0, 0.0)
        rights.append(right.astype(jnp.bfloat16))
    return lax.dot_general(
        jnp.concatenate(lefts, axis=1),
        jnp.concatenate(rights, axis=1),
        (((1,), (1,)), ((), ())),
        preferred_element_type=jnp.float32,
    )


def kernel(
    n,
    low_bits,
    relax_hbm,
    adjoint_ref,
    density_ref,
    velocity_ref,
    links_ref,
    patch_ref,
    owner_ref,
    out_ref,
    gradient_ref,
    first,
    second,
    rims_one,
    rims_two,
    rho,
    flow,
    bits,
    patch,
    owner,
    relax_ref,
    wall,
    sums,
    outgoing,
    incoming,
    local_sem,
    send_one,
    recv_one,
    send_two,
    recv_two,
    send_sum,
    recv_sum,
    met,
):
    me = lax.axis_index("span")
    above, below = lax.rem(me + 1, n), lax.rem(me + n - 1, n)
    ny = wall.shape[0]
    chunks = ny // ROWS

    def other(d):
        return lax.rem(me + d, n)

    pairs = [(relax_hbm, relax_ref)]
    pairs += [(adjoint_ref.at[j, 0], first.at[j, pl.ds(PAD, ny), :]) for j in range(19)]
    pairs += [(links_ref.at[i, 0], bits.at[i]) for i in range(2)]
    for level in (1, 0):
        pairs += [(velocity_ref.at[level, i, 0], flow.at[level, i]) for i in range(3)]
        pairs.append((density_ref.at[level, 0], rho.at[level]))
    pairs += [(patch_ref.at[0], patch), (owner_ref, owner)]
    loads = [
        pltpu.make_async_copy(source, target, local_sem.at[i])
        for i, (source, target) in enumerate(pairs)
    ]
    for load in loads:
        load.start()

    barrier = pltpu.get_barrier_semaphore()

    neighbours = (above, below) if n > 2 else (above,)
    for device in neighbours:
        pl.semaphore_signal(barrier, inc=1, device_id={"span": device}, device_id_type=MESH)
    for buffer in (first, second, rims_one, rims_two):
        blank = jnp.zeros((buffer.shape[0], PAD, buffer.shape[2]), jnp.float32)
        buffer[:, 0:PAD, :] = blank
        buffer[:, PAD + ny : PAD + ny + PAD, :] = blank
    pl.semaphore_wait(barrier, len(neighbours))

    pieces = PIECES
    length = ny // pieces
    ends_one = [length * (i + 1) for i in range(pieces)]
    ends_two = [end - ROWS for end in ends_one[:-1]] + [ny]
    ends_out = [end - ROWS for end in ends_two[:-1]] + [ny]

    def send_rims(sources, rims, sems, start, end):
        copies = []
        for i, (slots, source, target) in enumerate(sources(start, end)):
            copies.append(
                pltpu.make_async_remote_copy(
                    src_ref=source,
                    dst_ref=rims.at[slots, pl.ds(PAD + start, end - start), :],
                    send_sem=sems[0].at[i],
                    recv_sem=sems[1].at[i],
                    device_id={"span": target},
                    device_id_type=MESH,
                )
            )
        for copy in copies:
            copy.start()
        return copies

    def sources_one(start, end):
        rows = pl.ds(start, end - start)
        for k in range(5):
            yield k, adjoint_ref.at[RISING[k], 0, rows, :], below
            yield 5 + k, adjoint_ref.at[FALLING[k], 0, rows, :], above

    def sources_two(start, end):
        rows = pl.ds(PAD + start, end - start)
        yield pl.ds(0, 5), second.at[pl.ds(0, 5), rows, :], below
        yield pl.ds(5, 5), second.at[pl.ds(5, 5), rows, :], above

    def meet(i):
        far = 1 << i
        for side, device in enumerate((other(far), other(n - far))):
            pl.semaphore_signal(
                met.at[i, side], inc=1, device_id={"span": device}, device_id_type=MESH
            )

    def met_all(i):
        for side in range(2):
            pl.semaphore_wait(met.at[i, side], 1)

    copies_one = []
    for i, end in enumerate(ends_one):
        sems = (send_one.at[i], recv_one.at[i])
        copies_one.append(send_rims(sources_one, rims_one, sems, end - length, end))
    meet(0)
    for load in loads:
        load.wait()
    coefs = coefficients(relax_ref)

    def masks(rows):
        low, high = bits[0, rows, :], bits[1, rows, :]
        return [
            lax.bitwise_and(low if j < 10 else high, 1 << (j % 10)) != 0 for j in range(19)
        ]

    def walls(level, populations, place, add):
        def step(i, carry):
            start = pl.multiple_of(i * ROWS, ROWS)
            rows = pl.ds(start, ROWS)
            inner = pl.ds(pl.multiple_of(start + PAD, ROWS), ROWS)
            linked = masks(rows)
            u = [flow[level, axis, rows, :] for axis in range(3)]
            x = [
                jnp.where(linked[j], populations[place[OPPOSITE[j]], inner, :], 0.0) for j in range(19)
            ]
            value = wall_value(x, rho[level, rows, :], u, jnp.logical_not(linked[0]))
            wall[rows, :] = wall[rows, :] + value if add else value
            return carry

        lax.fori_loop(0, chunks, step, 0, unroll=4)

    def collisions(level, populations, place, rims, store, begin, end):
        def step(i, carry):
            start = pl.multiple_of(i * ROWS, ROWS)
            rows = pl.ds(start, ROWS)
            inner = pl.ds(pl.multiple_of(start + PAD, ROWS), ROWS)
            linked = masks(rows)
            u = [flow[level, axis, rows, :] for axis in range(3)]
            p = []
            for j, (step_x, step_y, step_z) in enumerate(VELOCITIES):
                shifted = inner if step_y == 0 else pl.ds(start + (PAD + step_y), ROWS)
                if step_x == 1:
                    upstream = rims[RISING.index(j), shifted, :]
                elif step_x == -1:
                    upstream = rims[5 + FALLING.index(j), shifted, :]
                else:
                    upstream = populations[place[j], shifted, :]
                if step_z != 0:
                    upstream = pltpu.roll(upstream, (-step_z) % upstream.shape[1], 1)
                p.append(jnp.where(linked[j], populations[place[OPPOSITE[j]], inner, :], upstream))
            for j, value in enumerate(collide(p, u, jnp.logical_not(linked[0]), coefs)):
                store(j, rows, inner, value)
            return carry

        lax.fori_loop(begin // ROWS, end // ROWS, step, 0, unroll=4)

    def store_second(j, rows, inner, value):
        second[PLACE[j], inner, :] = value

    walls(1, first, range(19), False)
    rounds = met.shape[0]
    for i in range(rounds):
        met_all(i)
        if i + 1 < rounds:
            meet(i + 1)
    copies_two = []
    for i, end in enumerate(ends_two):
        for copy in copies_one[i]:
            copy.wait_recv()
        start = ends_two[i - 1] if i else 0
        collisions(1, first, range(19), rims_one, store_second, start, end)
        sems = (send_two.at[i], recv_two.at[i])
        copies_two.append(send_rims(sources_two, rims_two, sems, start, end))

    walls(0, second, PLACE, True)

    def by_patch(i, total):
        rows = pl.ds(pl.multiple_of(i * ROWS, ROWS), ROWS)
        return total + one_hot_sums(patch[rows, :], wall[rows, :], 7, owner.shape[0])

    highs = owner.shape[0]
    total = lax.fori_loop(0, chunks, by_patch, jnp.zeros((3 * highs, 128), jnp.float32))
    sums[...] = total[:highs] + (total[highs : 2 * highs] + total[2 * highs :])

    targets = outgoing.shape[0] * outgoing.shape[1]

    def by_owner(i, total):
        rows = pl.ds(pl.multiple_of(i * ROWS, ROWS), ROWS)
        return total + one_hot_sums(owner[rows, :], sums[rows, :], low_bits, targets)

    total = lax.fori_loop(
        0, highs // ROWS, by_owner, jnp.zeros((3 * targets, 128), jnp.float32)
    )
    placed = total[:targets] + (total[targets : 2 * targets] + total[2 * targets :])
    per = outgoing.shape[1]
    for i in range(n):
        outgoing[i] = placed[i * per : (i + 1) * per]

    def sum_copy(d, source):
        return pltpu.make_async_remote_copy(
            src_ref=outgoing.at[other(d)],
            dst_ref=incoming.at[source],
            send_sem=send_sum.at[d],
            recv_sem=recv_sum.at[source],
            device_id={"span": other(d)},
            device_id_type=MESH,
        )

    def send(d, carry):
        sum_copy(d, me).start()
        return carry

    lax.fori_loop(1, n, send, 0)

    def store_out(j, rows, inner, value):
        out_ref[j, 0, rows, :] = value

    for i, end in enumerate(ends_out):
        for copy in copies_two[i]:
            copy.wait_recv()
        start = ends_out[i - 1] if i else 0
        collisions(0, second, PLACE, rims_two, store_out, start, end)

    def collect(d, total):
        source = other(n - d)
        sum_copy(d, source).wait_recv()
        return total + incoming[source]

    gradient_ref[...] = lax.fori_loop(1, n, collect, outgoing[me])

    def sent(d, carry):
        sum_copy(d, me).wait_send()
        return carry

    lax.fori_loop(1, n, sent, 0)
    for copies in copies_one + copies_two:
        for copy in copies:
            copy.wait_send()


def body(n, adjoint_in, density, velocity, links, patch_map, owner, relax):
    _, planes, ny, nz = adjoint_in.shape
    assert planes == 1 and nz == 128 and ny % ROWS == 0
    rows = owner.shape[0] // n
    low = min(128, rows)
    per = rows // low
    highs = owner.shape[0] // 128
    padded = ny + 2 * PAD
    hbm = pl.BlockSpec(memory_space=pltpu.HBM)
    vmem = pl.BlockSpec(memory_space=pltpu.VMEM)
    levels = density.shape[0]
    rounds = max(1, (n // 2 - 1).bit_length())
    adjoint, gradient = pl.pallas_call(
        functools.partial(kernel, n, low.bit_length() - 1),
        out_shape=(
            pltpu.VMEM(adjoint_in.shape, jnp.float32),
            pltpu.VMEM((per, 128), jnp.float32),
        ),
        in_specs=[hbm] * 7,
        out_specs=(vmem, vmem),
        scratch_shapes=[
            pltpu.VMEM((19, padded, nz), jnp.float32),
            pltpu.VMEM((19, padded, nz), jnp.float32),
            pltpu.VMEM((10, padded, nz), jnp.float32),
            pltpu.VMEM((10, padded, nz), jnp.float32),
            pltpu.VMEM((levels, ny, nz), jnp.float32),
            pltpu.VMEM((levels, 3, ny, nz), jnp.float32),
            pltpu.VMEM((2, ny, nz), jnp.int32),
            pltpu.VMEM((ny, nz), jnp.int32),
            pltpu.VMEM((highs, 128), jnp.int32),
            pltpu.SMEM(relax.shape, jnp.float32),
            pltpu.VMEM((ny, nz), jnp.float32),
            pltpu.VMEM((highs, 128), jnp.float32),
            pltpu.VMEM((n, per, 128), jnp.float32),
            pltpu.VMEM((n, per, 128), jnp.float32),
            pltpu.SemaphoreType.DMA((32,)),
            pltpu.SemaphoreType.DMA((PIECES, 10)),
            pltpu.SemaphoreType.DMA((PIECES, 10)),
            pltpu.SemaphoreType.DMA((PIECES, 2)),
            pltpu.SemaphoreType.DMA((PIECES, 2)),
            pltpu.SemaphoreType.DMA((n,)),
            pltpu.SemaphoreType.DMA((n,)),
            pltpu.SemaphoreType.REGULAR((rounds, 2)),
        ],
        compiler_params=pltpu.CompilerParams(
            collective_id=0, has_side_effects=True, vmem_limit_bytes=60 * 1024 * 1024
        ),
        cost_estimate=pl.CostEstimate(
            flops=40_000_000, bytes_accessed=4_000_000, transcendentals=0
        ),
    )(relax, adjoint_in, density, velocity, links, patch_map, owner.reshape(highs, 128))
    return adjoint, gradient[:, :low].reshape(rows)


def solution(mesh):
    in_specs = (
        P("case", "span", None, None),
        P("case", "span", None, None),
        P("case", None, "span", None, None),
        P(None, ("case", "span"), None, None),
        P(("case", "span"), None, None),
        P(),
        P("case"),
    )
    out_specs = (P("case", "span", None, None), P(("case", "span")))
    return jax.shard_map(
        functools.partial(body, mesh.shape["span"]),
        mesh=mesh,
        in_specs=in_specs,
        out_specs=out_specs,
        check_vma=False,
    )
```

```python
import functools

import jax
import jax.numpy as jnp
import numpy as np
from jax import lax
from jax.experimental import pallas as pl
from jax.experimental.pallas import tpu as pltpu
from jax.sharding import PartitionSpec as P

MESH = pl.DeviceIdType.MESH
RISING = (1, 7, 9, 11, 13)
FALLING = (2, 8, 10, 12, 14)
OPPOSITE = (0, 2, 1, 4, 3, 6, 5, 8, 7, 10, 9, 12, 11, 14, 13, 16, 15, 18, 17)
VELOCITIES = (
    (0, 0, 0),
    (1, 0, 0),
    (-1, 0, 0),
    (0, 1, 0),
    (0, -1, 0),
    (0, 0, 1),
    (0, 0, -1),
    (1, 1, 0),
    (-1, -1, 0),
    (1, -1, 0),
    (-1, 1, 0),
    (1, 0, 1),
    (-1, 0, -1),
    (1, 0, -1),
    (-1, 0, 1),
    (0, 1, 1),
    (0, -1, -1),
    (0, 1, -1),
    (0, -1, 1),
)
PAD = 8
ROWS = 8
PIECES = 1
ORDER = RISING + FALLING + (0, 3, 4, 5, 6, 15, 16, 17, 18)
PLACE = tuple(ORDER.index(j) for j in range(19))


def moment_table():
    lattice = np.asarray(VELOCITIES, np.float32)
    x, y, z = lattice[:, 0], lattice[:, 1], lattice[:, 2]
    monomials = [np.ones((19,), np.float32), x, y, z, x * y, x * z, y * z, x * x, y * y, z * z]
    monomials += [x * y * y, x * z * z, y * x * x, z * x * x, y * z * z, z * y * y]
    monomials += [x * x * y * y, x * x * z * z, y * y * z * z]
    basis = []
    for vector in monomials:
        for sweep in range(2):
            for earlier in basis:
                vector = vector - np.sum(vector * earlier) * earlier
        basis.append(vector / np.sqrt(np.sum(vector * vector)))
    return np.stack(basis)


TABLE = moment_table()
EVEN_AT = (0, 1, 3, 5, 7, 11, 15)
EVEN_ROWS = (7, 8, 9, 16, 17, 18)
ODD_AT = ((1, 7, 11), (3, 7, 15), (5, 11, 15))
ODD_ROWS = ((10, 11), (12, 14), (13, 15))
MIXED = ((4, 7), (5, 11), (6, 15))


def coefficients(relax_ref):
    def block(at, rows):
        rates = [relax_ref[row] for row in rows]
        out = {}
        for a in range(len(at)):
            for b in range(a, len(at)):
                total = None
                for row, rate in zip(rows, rates):
                    factor = float(TABLE[row, at[a]]) * float(TABLE[row, at[b]])
                    if abs(factor) < 1e-6:
                        continue
                    term = rate * np.float32(factor)
                    total = term if total is None else total + term
                out[a, b] = out[b, a] = total
        return out

    even = block(EVEN_AT, EVEN_ROWS)
    odd = [block(at, rows) for at, rows in zip(ODD_AT, ODD_ROWS)]
    mixed = [relax_ref[row] * np.float32(float(TABLE[row, at]) ** 2) for row, at in MIXED]
    return even, odd, mixed


def apply(block, values):
    result = []
    for a in range(len(values)):
        total = None
        for b, value in enumerate(values):
            if block[a, b] is None:
                continue
            term = block[a, b] * value
            total = term if total is None else total + term
        result.append(total)
    return result


def classes(p):
    even = [p[0], p[1] + p[2], p[3] + p[4], p[5] + p[6]]
    single = [p[1] - p[2], p[3] - p[4], p[5] - p[6]]
    mixed, firsts, seconds = [], [], []
    for base in (7, 11, 15):
        a, b = p[base] + p[base + 1], p[base + 2] + p[base + 3]
        c, d = p[base] - p[base + 1], p[base + 2] - p[base + 3]
        even.append(a + b)
        mixed.append(a - b)
        firsts.append(c + d)
        seconds.append(c - d)
    odd = [
        [single[0], firsts[0], firsts[1]],
        [single[1], seconds[0], firsts[2]],
        [single[2], seconds[1], seconds[2]],
    ]
    return even, odd, mixed


def quadratic(diagonal, mixed, u):
    xx, yy, zz = diagonal
    xy, xz, yz = mixed
    return (
        u[0] * xx + u[1] * xy + u[2] * xz,
        u[0] * xy + u[1] * yy + u[2] * yz,
        u[0] * xz + u[1] * yz + u[2] * zz,
    )


def collide(p, u, fluid, coefs):
    even_block, odd_block, mixed_block = coefs
    even, odd, mixed = classes(p)
    ge = apply(even_block, even)
    go = [apply(block, values) for block, values in zip(odd_block, odd)]
    gm = [scale * value for scale, value in zip(mixed_block, mixed)]
    w0, w1, w2 = np.float32(1 / 3), np.float32(2 / 18), np.float32(4 / 36)
    axes = [w1 * value for value in ge[1:4]]
    planes = [w2 * value for value in ge[4:7]]
    diagonal = (
        axes[0] + (planes[0] + planes[1]),
        axes[1] + (planes[0] + planes[2]),
        axes[2] + (planes[1] + planes[2]),
    )
    total = w0 * ge[0] + (axes[0] + axes[1] + axes[2]) + (planes[0] + planes[1] + planes[2])
    first = [w1 * value[0] + w2 * (value[1] + value[2]) for value in go]
    cross = [w2 * value for value in gm]
    bent = quadratic(diagonal, cross, u)
    speed_sq = u[0] * u[0] + u[1] * u[1] + u[2] * u[2]
    s0 = total * (1.0 + 1.5 * speed_sq) - 4.5 * (u[0] * bent[0] + u[1] * bent[1] + u[2] * bent[2])
    s = [3.0 * (first[i] + 3.0 * bent[i] - u[i] * total) for i in range(3)]
    he = [s0 - value for value in ge]
    ho = [[s[i] - value for value in go[i]] for i in range(3)]
    out = [None] * 19
    out[0] = p[0] + he[0]
    for i in range(3):
        out[1 + 2 * i] = p[1 + 2 * i] + (he[1 + i] + ho[i][0])
        out[2 + 2 * i] = p[2 + 2 * i] + (he[1 + i] - ho[i][0])
    pairs = ((ho[0][1], ho[1][1]), (ho[0][2], ho[2][1]), (ho[1][2], ho[2][2]))
    for i, (left, right) in enumerate(pairs):
        base = 7 + 4 * i
        e, f = he[4 + i] - gm[i], he[4 + i] + gm[i]
        x, y = left + right, left - right
        out[base] = p[base] + (e + x)
        out[base + 1] = p[base + 1] + (e - x)
        out[base + 2] = p[base + 2] + (f + y)
        out[base + 3] = p[base + 3] + (f - y)
    return [jnp.where(fluid, value, 0.0) for value in out]


def wall_value(x, rho, u, fluid):
    even, odd, mixed = classes(x)
    total = sum(even[1:], even[0])
    diagonal = (
        even[1] + (even[4] + even[5]),
        even[2] + (even[4] + even[6]),
        even[3] + (even[5] + even[6]),
    )
    first = [value[0] + (value[1] + value[2]) for value in odd]
    bent = quadratic(diagonal, mixed, u)
    speed_sq = u[0] * u[0] + u[1] * u[1] + u[2] * u[2]
    linear = [3.0 * first[i] + 4.5 * bent[i] for i in range(3)]
    value = total * (1.0 - 1.5 * speed_sq) + (
        u[0] * linear[0] + u[1] * linear[1] + u[2] * linear[2]
    )
    return jnp.where(fluid, rho * value, 0.0)


def split3(value):
    one = value.astype(jnp.bfloat16)
    rest = value - one.astype(jnp.float32)
    two = rest.astype(jnp.bfloat16)
    three = (rest - two.astype(jnp.float32)).astype(jnp.bfloat16)
    return [part.astype(jnp.float32) for part in (one, two, three)]


def one_hot_sums(index, value, low_bits, highs):
    high = lax.shift_right_logical(index, low_bits)
    low = lax.bitwise_and(index, (1 << low_bits) - 1)
    parts = split3(value)
    high_iota = lax.broadcasted_iota(jnp.int32, (highs, 128), 0)
    low_iota = lax.broadcasted_iota(jnp.int32, (128, 128), 0)
    lefts, rights = [], []
    for row in range(ROWS):
        hit = high_iota == high[row : row + 1, :]
        left = [jnp.where(hit, part[row : row + 1, :], 0.0) for part in parts]
        lefts.append(jnp.concatenate(left, axis=0).astype(jnp.bfloat16))
        right = jnp.where(low_iota == low[row : row + 1, :], 1.0, 0.0)
        rights.append(right.astype(jnp.bfloat16))
    return lax.dot_general(
        jnp.concatenate(lefts, axis=1),
        jnp.concatenate(rights, axis=1),
        (((1,), (1,)), ((), ())),
        preferred_element_type=jnp.float32,
    )


def kernel(
    n,
    low_bits,
    relax_hbm,
    adjoint_ref,
    density_ref,
    velocity_ref,
    links_ref,
    patch_ref,
    owner_ref,
    out_ref,
    gradient_ref,
    first,
    second,
    rims_one,
    rims_two,
    rho,
    flow,
    bits,
    patch,
    owner,
    relax_ref,
    wall,
    sums,
    outgoing,
    incoming,
    local_sem,
    send_one,
    recv_one,
    send_two,
    recv_two,
    send_sum,
    recv_sum,
    met,
):
    me = lax.axis_index("span")
    above, below = lax.rem(me + 1, n), lax.rem(me + n - 1, n)
    ny = wall.shape[0]
    chunks = ny // ROWS

    def other(d):
        return lax.rem(me + d, n)

    pairs = [(relax_hbm, relax_ref)]
    pairs += [(adjoint_ref.at[j, 0], first.at[j, pl.ds(PAD, ny), :]) for j in range(19)]
    pairs += [(links_ref.at[i, 0], bits.at[i]) for i in range(2)]
    for level in (1, 0):
        pairs += [(velocity_ref.at[level, i, 0], flow.at[level, i]) for i in range(3)]
        pairs.append((density_ref.at[level, 0], rho.at[level]))
    pairs += [(patch_ref.at[0], patch), (owner_ref, owner)]
    loads = [
        pltpu.make_async_copy(source, target, local_sem.at[i])
        for i, (source, target) in enumerate(pairs)
    ]
    for load in loads:
        load.start()

    barrier = pltpu.get_barrier_semaphore()

    neighbours = (above, below) if n > 2 else (above,)
    for device in neighbours:
        pl.semaphore_signal(barrier, inc=1, device_id={"span": device}, device_id_type=MESH)
    for buffer in (first, second, rims_one, rims_two):
        blank = jnp.zeros((buffer.shape[0], PAD, buffer.shape[2]), jnp.float32)
        buffer[:, 0:PAD, :] = blank
        buffer[:, PAD + ny : PAD + ny + PAD, :] = blank
    pl.semaphore_wait(barrier, len(neighbours))

    pieces = PIECES
    length = ny // pieces
    ends_one = [length * (i + 1) for i in range(pieces)]
    ends_two = [end - ROWS for end in ends_one[:-1]] + [ny]
    ends_out = [end - ROWS for end in ends_two[:-1]] + [ny]

    def send_rims(sources, rims, sems, start, end):
        copies = []
        for i, (slots, source, target) in enumerate(sources(start, end)):
            copies.append(
                pltpu.make_async_remote_copy(
                    src_ref=source,
                    dst_ref=rims.at[slots, pl.ds(PAD + start, end - start), :],
                    send_sem=sems[0].at[i],
                    recv_sem=sems[1].at[i],
                    device_id={"span": target},
                    device_id_type=MESH,
                )
            )
        for copy in copies:
            copy.start()
        return copies

    def sources_one(start, end):
        rows = pl.ds(start, end - start)
        for k in range(5):
            yield k, adjoint_ref.at[RISING[k], 0, rows, :], below
            yield 5 + k, adjoint_ref.at[FALLING[k], 0, rows, :], above

    def sources_two(start, end):
        rows = pl.ds(PAD + start, end - start)
        yield pl.ds(0, 5), second.at[pl.ds(0, 5), rows, :], below
        yield pl.ds(5, 5), second.at[pl.ds(5, 5), rows, :], above

    def meet(i):
        far = 1 << i
        for side, device in enumerate((other(far), other(n - far))):
            pl.semaphore_signal(
                met.at[i, side], inc=1, device_id={"span": device}, device_id_type=MESH
            )

    def met_all(i):
        for side in range(2):
            pl.semaphore_wait(met.at[i, side], 1)

    copies_one = []
    for i, end in enumerate(ends_one):
        sems = (send_one.at[i], recv_one.at[i])
        copies_one.append(send_rims(sources_one, rims_one, sems, end - length, end))
    meet(0)
    for load in loads:
        load.wait()
    coefs = coefficients(relax_ref)

    def masks(rows):
        low, high = bits[0, rows, :], bits[1, rows, :]
        return [
            lax.bitwise_and(low if j < 10 else high, 1 << (j % 10)) != 0 for j in range(19)
        ]

    def walls(level, populations, place, add):
        def step(i, carry):
            start = pl.multiple_of(i * ROWS, ROWS)
            rows = pl.ds(start, ROWS)
            inner = pl.ds(pl.multiple_of(start + PAD, ROWS), ROWS)
            linked = masks(rows)
            u = [flow[level, axis, rows, :] for axis in range(3)]
            x = [
                jnp.where(linked[j], populations[place[OPPOSITE[j]], inner, :], 0.0) for j in range(19)
            ]
            value = wall_value(x, rho[level, rows, :], u, jnp.logical_not(linked[0]))
            wall[rows, :] = wall[rows, :] + value if add else value
            return carry

        lax.fori_loop(0, chunks, step, 0, unroll=4)

    def collisions(level, populations, place, rims, store, begin, end):
        def step(i, carry):
            start = pl.multiple_of(i * ROWS, ROWS)
            rows = pl.ds(start, ROWS)
            inner = pl.ds(pl.multiple_of(start + PAD, ROWS), ROWS)
            linked = masks(rows)
            u = [flow[level, axis, rows, :] for axis in range(3)]
            p = []
            for j, (step_x, step_y, step_z) in enumerate(VELOCITIES):
                shifted = inner if step_y == 0 else pl.ds(start + (PAD + step_y), ROWS)
                if step_x == 1:
                    upstream = rims[RISING.index(j), shifted, :]
                elif step_x == -1:
                    upstream = rims[5 + FALLING.index(j), shifted, :]
                else:
                    upstream = populations[place[j], shifted, :]
                if step_z != 0:
                    upstream = pltpu.roll(upstream, (-step_z) % upstream.shape[1], 1)
                p.append(jnp.where(linked[j], populations[place[OPPOSITE[j]], inner, :], upstream))
            for j, value in enumerate(collide(p, u, jnp.logical_not(linked[0]), coefs)):
                store(j, rows, inner, value)
            return carry

        lax.fori_loop(begin // ROWS, end // ROWS, step, 0, unroll=4)

    def store_second(j, rows, inner, value):
        second[PLACE[j], inner, :] = value

    walls(1, first, range(19), False)
    rounds = met.shape[0]
    for i in range(rounds):
        met_all(i)
        if i + 1 < rounds:
            meet(i + 1)
    copies_two = []
    for i, end in enumerate(ends_two):
        for copy in copies_one[i]:
            copy.wait_recv()
        start = ends_two[i - 1] if i else 0
        collisions(1, first, range(19), rims_one, store_second, start, end)
        sems = (send_two.at[i], recv_two.at[i])
        copies_two.append(send_rims(sources_two, rims_two, sems, start, end))

    walls(0, second, PLACE, True)

    def by_patch(i, total):
        rows = pl.ds(pl.multiple_of(i * ROWS, ROWS), ROWS)
        return total + one_hot_sums(patch[rows, :], wall[rows, :], 7, owner.shape[0])

    highs = owner.shape[0]
    total = lax.fori_loop(0, chunks, by_patch, jnp.zeros((3 * highs, 128), jnp.float32), unroll=2)
    sums[...] = total[:highs] + (total[highs : 2 * highs] + total[2 * highs :])

    targets = outgoing.shape[0] * outgoing.shape[1]

    def by_owner(i, total):
        rows = pl.ds(pl.multiple_of(i * ROWS, ROWS), ROWS)
        return total + one_hot_sums(owner[rows, :], sums[rows, :], low_bits, targets)

    total = lax.fori_loop(
        0, highs // ROWS, by_owner, jnp.zeros((3 * targets, 128), jnp.float32), unroll=True
    )
    placed = total[:targets] + (total[targets : 2 * targets] + total[2 * targets :])
    per = outgoing.shape[1]
    for i in range(n):
        outgoing[i] = placed[i * per : (i + 1) * per]

    def sum_copy(d, source):
        return pltpu.make_async_remote_copy(
            src_ref=outgoing.at[other(d)],
            dst_ref=incoming.at[source],
            send_sem=send_sum.at[d],
            recv_sem=recv_sum.at[source],
            device_id={"span": other(d)},
            device_id_type=MESH,
        )

    def send(d, carry):
        sum_copy(d, me).start()
        return carry

    lax.fori_loop(1, n, send, 0, unroll=n < 32)

    def store_out(j, rows, inner, value):
        out_ref[j, 0, rows, :] = value

    for i, end in enumerate(ends_out):
        for copy in copies_two[i]:
            copy.wait_recv()
        start = ends_out[i - 1] if i else 0
        collisions(0, second, PLACE, rims_two, store_out, start, end)

    def collect(d, total):
        source = other(n - d)
        sum_copy(d, source).wait_recv()
        return total + incoming[source]

    gradient_ref[...] = lax.fori_loop(1, n, collect, outgoing[me], unroll=n < 32)

    def sent(d, carry):
        sum_copy(d, me).wait_send()
        return carry

    lax.fori_loop(1, n, sent, 0, unroll=n < 32)
    for copies in copies_one + copies_two:
        for copy in copies:
            copy.wait_send()


def body(n, adjoint_in, density, velocity, links, patch_map, owner, relax):
    _, planes, ny, nz = adjoint_in.shape
    assert planes == 1 and nz == 128 and ny % ROWS == 0
    rows = owner.shape[0] // n
    low = min(128, rows)
    per = rows // low
    highs = owner.shape[0] // 128
    padded = ny + 2 * PAD
    hbm = pl.BlockSpec(memory_space=pltpu.HBM)
    vmem = pl.BlockSpec(memory_space=pltpu.VMEM)
    levels = density.shape[0]
    rounds = max(1, (n // 2 - 1).bit_length())
    adjoint, gradient = pl.pallas_call(
        functools.partial(kernel, n, low.bit_length() - 1),
        out_shape=(
            pltpu.VMEM(adjoint_in.shape, jnp.float32),
            pltpu.VMEM((per, 128), jnp.float32),
        ),
        in_specs=[hbm] * 7,
        out_specs=(vmem, vmem),
        scratch_shapes=[
            pltpu.VMEM((19, padded, nz), jnp.float32),
            pltpu.VMEM((19, padded, nz), jnp.float32),
            pltpu.VMEM((10, padded, nz), jnp.float32),
            pltpu.VMEM((10, padded, nz), jnp.float32),
            pltpu.VMEM((levels, ny, nz), jnp.float32),
            pltpu.VMEM((levels, 3, ny, nz), jnp.float32),
            pltpu.VMEM((2, ny, nz), jnp.int32),
            pltpu.VMEM((ny, nz), jnp.int32),
            pltpu.VMEM((highs, 128), jnp.int32),
            pltpu.SMEM(relax.shape, jnp.float32),
            pltpu.VMEM((ny, nz), jnp.float32),
            pltpu.VMEM((highs, 128), jnp.float32),
            pltpu.VMEM((n, per, 128), jnp.float32),
            pltpu.VMEM((n, per, 128), jnp.float32),
            pltpu.SemaphoreType.DMA((32,)),
            pltpu.SemaphoreType.DMA((PIECES, 10)),
            pltpu.SemaphoreType.DMA((PIECES, 10)),
            pltpu.SemaphoreType.DMA((PIECES, 2)),
            pltpu.SemaphoreType.DMA((PIECES, 2)),
            pltpu.SemaphoreType.DMA((n,)),
            pltpu.SemaphoreType.DMA((n,)),
            pltpu.SemaphoreType.REGULAR((rounds, 2)),
        ],
        compiler_params=pltpu.CompilerParams(
            collective_id=0, has_side_effects=True, vmem_limit_bytes=60 * 1024 * 1024
        ),
        cost_estimate=pl.CostEstimate(
            flops=40_000_000, bytes_accessed=4_000_000, transcendentals=0
        ),
    )(relax, adjoint_in, density, velocity, links, patch_map, owner.reshape(highs, 128))
    return adjoint, gradient[:, :low].reshape(rows)


def solution(mesh):
    in_specs = (
        P("case", "span", None, None),
        P("case", "span", None, None),
        P("case", None, "span", None, None),
        P(None, ("case", "span"), None, None),
        P(("case", "span"), None, None),
        P(),
        P("case"),
    )
    out_specs = (P("case", "span", None, None), P(("case", "span")))
    return jax.shard_map(
        functools.partial(body, mesh.shape["span"]),
        mesh=mesh,
        in_specs=in_specs,
        out_specs=out_specs,
        check_vma=False,
    )
```
